32 devices in a mesh: dp: 4 (over z), expert: 8 (over y, x, core).
Axes of the slice: x: 2, y: 2, z: 4, core: 2. Of those that a mesh axis runs over, the one named last changes fastest.
Arguments:
- tokens: bfloat16 [8192, 1024], P(('dp', 'expert')), may hold values from -6 to 6
- routes: int32 [8192, 8], P(('dp', 'expert')), may hold values from 0 to 31, all different within a row; in each aligned block of 256 rows (0 to 255, 256 to 511, ...) at most 128 rows name the same one
- lengths: int32 [32, 4], P(('dp', 'expert')), may hold values from 1 to 192, 256 in all within a row
- query_weight: bfloat16 [1024, 1024], P('dp'), may hold values from -0.1875 to 0.1875
- key_weight: bfloat16 [1024, 512], P('dp'), may hold values from -0.1875 to 0.1875
- value_weight: bfloat16 [1024, 512], P('dp'), may hold values from -0.1875 to 0.1875
- output_weight: bfloat16 [1024, 1024], P('dp'), may hold values from -1 to 1
- router_weight: bfloat16 [1024, 32], P('dp'), may hold values from -0.09375 to 0.09375
- first_gain: bfloat16 [1024], P('dp'), may hold values from 0.5 to 1.5
- second_gain: bfloat16 [1024], P('dp'), may hold values from 0.5 to 1.5
- expert_gate: bfloat16 [32, 1024, 512], P('expert', 'dp'), may hold values from -0.1875 to 0.1875
- expert_up: bfloat16 [32, 1024, 512], P('expert', 'dp'), may hold values from -0.1875 to 0.1875
- expert_down: bfloat16 [32, 512, 1024], P('expert', None, 'dp'), may hold values from -1 to 1
- cotangent: bfloat16 [8192, 1024], P(('dp', 'expert')), may hold values from -6 to 6
Outputs:
- output: bfloat16 [8192, 1024], P(('dp', 'expert'))
- input_grad: float32 [8192, 1024], P(('dp', 'expert'))
- query_grad: float32 [1024, 1024], P('dp')
- key_grad: float32 [1024, 512], P('dp')
- value_grad: float32 [1024, 512], P('dp')
- output_grad: float32 [1024, 1024], P('dp')
- router_grad: float32 [1024, 32], P('dp')
- first_gain_grad: float32 [1024], P('dp')
- second_gain_grad: float32 [1024], P('dp')
- gate_grad: float32 [32, 1024, 512], P('expert', 'dp')
- up_grad: float32 [32, 1024, 512], P('expert', 'dp')
- down_grad: float32 [32, 512, 1024], P('expert', None, 'dp')
The draws below stay inside these ranges and needn't reach their ends.
Inputs may be any that keep to these rules, and one draw needn't show every extreme that they name: `routes`: among the 256 rows of one device no expert is named more than 128 times, a bound that some block reaches; a row names 8 different experts. `lengths`: each row sums to 256; the largest length is 192.
All inputs are finite; a program needn't handle non-finite values.
Results may differ from the reference program's by a relative error of at most 0.02.
Values may be sent and summed in bfloat16 or wider, within the bound.
No kernel may reach another device: no remote copies, remote signals or barrier semaphores. Data moves between devices by JAX's collectives and lax.ppermute only.
A program may use at most 192 MiB of HBM per device.

```python
import math
import jax
import jax.numpy as jnp
import numpy as np
from jax import lax

D = 1024
HEADS = 16
KV_HEADS = 8
HEAD_DIM = 64
EXPERTS = 32
TOPK = 8
FF = 512
TOK_DEV = 256
SEQS_DEV = 4
MOST_LEN = 192
CAP = 128
HD = 1024
KVD = 512
TOKENS = 8192
N_DP = 4
N_EXPERT = 8


def level_of(rng, dims, cuts, least, top_value):
    level = 1.0
    for axis_at, parts in cuts:
        steps = jax.random.uniform(jax.random.fold_in(jax.random.fold_in(rng, 6), axis_at), (parts,), jnp.float32, least / len(cuts), top_value / len(cuts))
        level = level * jnp.repeat(jnp.exp(steps), dims[axis_at] // parts).reshape((-1,) + (1,) * (len(dims) - 1 - axis_at))
    return level


def profile(count, total, most, lean):
    loads = [(1 << 20) // math.isqrt(standing ** lean) + 1 for standing in range(2, count + 1)]
    rest, counts = total - most - (count - 1), [1] * (count - 1)
    while rest > 0:
        movable = [i for i in range(count - 1) if counts[i] < most]
        mass, budget = sum([loads[i] for i in movable]), rest
        for i in movable:
            extra = min(most - counts[i], max(1, budget * loads[i] // mass), rest)
            counts[i] = counts[i] + extra
            rest = rest - extra
    return np.array([most] + counts)


def uneven(rng, amount, total, bound, slope):
    if amount == 2:
        one = jax.random.randint(rng, (), max(1, total - bound), min(bound, total - 1) + 1)
        return jnp.stack([one, total - one])
    sizes = jnp.asarray(profile(amount, total, bound, slope), jnp.int32)
    twos = (amount - 1) // 2
    donor, taker = sizes[1:1 + 2 * twos:2], sizes[2:2 + 2 * twos:2]
    margin = jnp.minimum(donor - 1, bound - taker)
    moved = jax.random.randint(jax.random.fold_in(rng, 1), (twos,), 0, 1 << 20) % (margin + 1)
    sizes = sizes.at[1:1 + 2 * twos:2].set(donor - moved).at[2:2 + 2 * twos:2].set(taker + moved)
    return sizes[jax.random.permutation(jax.random.fold_in(rng, 2), amount)]


def deal_out(stream_key, own, number, rows, count, top, reach, lean):
    sequence = jax.random.permutation(stream_key, count)
    heavy_load, ordinary = shares(count, rows * top, reach, lean, True), shares(count, rows * top, reach, lean, False)
    places = jnp.arange(count)

    def named(sizes, turn):
        used = int((sizes > 0).sum())
        fixed = max(1, used // 4)
        moved = fixed + (places - fixed + turn * (used - fixed)) % max(1, count - fixed)
        return jnp.zeros((count,), jnp.int32).at[sequence[jnp.where(places < fixed, places, moved)]].set(jnp.asarray(sizes, jnp.int32))

    sizes = jnp.where(number % 4 == 0, named(heavy_load, number // 4), named(ordinary, number - number // 4 - 1))
    mixed = jax.random.permutation(jax.random.fold_in(own, 3), count)
    giver, receiver = mixed[0:count // 2 * 2:2], mixed[1:count // 2 * 2:2]
    margin = jnp.minimum(sizes[giver] - 1, reach - sizes[receiver]) // 2
    margin = jnp.where((giver == sequence[0]) | (receiver == sequence[0]) | (sizes[receiver] == 0), 0, jnp.maximum(margin, 0))
    moved = jax.random.randint(jax.random.fold_in(own, 4), (count // 2,), 0, 1 << 20) % (margin + 1)
    sizes = sizes.at[giver].add(-moved).at[receiver].add(moved)
    members = jnp.searchsorted(jnp.cumsum(sizes), jnp.arange(rows * top), side="right").astype(jnp.int32)
    grid = members.reshape(top, rows).T
    grid = grid[jax.random.permutation(jax.random.fold_in(own, 1), rows)]
    turn = jax.random.randint(jax.random.fold_in(own, 2), (rows, 1), 0, top)
    return jnp.take_along_axis(grid, (jnp.arange(top)[None, :] + turn) % top, axis=1)


def shares(number_of, total, reach, lean, full):
    portions = [(1 << 20) // math.isqrt(rank ** lean) + 1 for rank in range(1, number_of + 1)]
    largest = reach if full else min(reach, max(-(-total // number_of), total * portions[0] // sum(portions)))
    least = 1 if total - largest >= number_of - 1 else 0
    given, spare = [largest] + [least] * (number_of - 1), total - largest - least * (number_of - 1)
    while spare > 0:
        movable = [i for i in range(1, number_of) if given[i] < largest] or [i for i in range(1, number_of) if given[i] < reach]
        mass, left = sum([portions[i] for i in movable]), spare
        for i in movable:
            extra = min(reach - given[i], max(1, left * portions[i] // mass), spare)
            given[i] = given[i] + extra
            spare = spare - extra
    return np.array(given)


def normal_values(stream_key, shape, scale, most, shards=(), held_as=jnp.bfloat16):
    drawn = jax.random.normal(stream_key, shape, jnp.float32) * scale
    if len(shards) > 0:
        drawn = level_of(stream_key, shape, shards, -0.22, 0.18) * drawn
    return jnp.clip(drawn, min=-most, max=most).astype(held_as)


def setup_inputs(seed: int = 0) -> dict:
    seeds = jax.random.split(jax.random.key(seed), 15)
    tokens = normal_values(seeds[0], (TOKENS, D), 1.0, 6.0, ((0, 32),))
    routes_keys = jax.random.split(jax.random.fold_in(seeds[1], 1), TOKENS // TOK_DEV)
    routes_turns = jax.random.permutation(jax.random.fold_in(seeds[1], 3), TOKENS // TOK_DEV)
    routes = jax.vmap(lambda own, number: deal_out(jax.random.fold_in(seeds[1], 2), own, number, TOK_DEV, EXPERTS, TOPK, CAP, 2))(routes_keys, routes_turns).reshape((TOKENS, TOPK))
    lengths = jax.vmap(lambda own: uneven(own, SEQS_DEV, TOK_DEV, MOST_LEN, 2))(jax.random.split(seeds[2], (N_DP * N_EXPERT))).reshape((N_DP * N_EXPERT, SEQS_DEV)).astype(jnp.int32)
    query_weight = normal_values(seeds[3], (D, HD), D ** -0.5, 0.1875, ((0, 4),))
    key_weight = normal_values(seeds[4], (D, KVD), D ** -0.5, 0.1875, ((0, 4),))
    value_weight = normal_values(seeds[5], (D, KVD), D ** -0.5, 0.1875, ((0, 4),))
    output_weight = normal_values(seeds[6], (HD, D), (HD // 32) ** -0.5, 1.0, ((0, 4),))
    router_weight = normal_values(seeds[7], (D, EXPERTS), (4 * D) ** -0.5, 0.09375, ((0, 4),))
    first_gain = jnp.clip(1.0 + 0.1 * jax.random.normal(seeds[8], (D,), jnp.float32), 0.5, 1.5).astype(jnp.bfloat16)
    second_gain = jnp.clip(1.0 + 0.1 * jax.random.normal(seeds[9], (D,), jnp.float32), 0.5, 1.5).astype(jnp.bfloat16)
    expert_gate = normal_values(seeds[10], (EXPERTS, D, FF), D ** -0.5, 0.1875, ((0, 8), (1, 4)))
    expert_up = normal_values(seeds[11], (EXPERTS, D, FF), D ** -0.5, 0.1875, ((0, 8), (1, 4)))
    expert_down = normal_values(seeds[12], (EXPERTS, FF, D), (FF // 16) ** -0.5, 1.0, ((0, 8), (2, 4)))
    cotangent = normal_values(seeds[13], (TOKENS, D), 1.0, 6.0, ((0, 32),))
    return {"tokens": tokens, "routes": routes, "lengths": lengths, "query_weight": query_weight, "key_weight": key_weight, "value_weight": value_weight, "output_weight": output_weight, "router_weight": router_weight, "first_gain": first_gain, "second_gain": second_gain, "expert_gate": expert_gate, "expert_up": expert_up, "expert_down": expert_down, "cotangent": cotangent}


@jax.custom_vjp
def low(v):
    return lax.optimization_barrier(v.astype(jnp.bfloat16)).astype(jnp.float32)

@jax.custom_vjp
def low_back(v):
    return v

def low_keep(v):
    return (low(v), None)

def low_pass(kept, grad):
    return (grad,)

def back_keep(v):
    return (v, None)

def back_low(kept, grad):
    return (low(grad),)
low.defvjp(low_keep, low_pass)
low_back.defvjp(back_keep, back_low)
EPSILON = 1e-06
THETA = 10000.0
PRECISE = lax.Precision.HIGHEST

def normalize(values, weights):
    return values * lax.rsqrt(lax.optimization_barrier(jnp.mean(values * values, axis=-1, keepdims=True)) + EPSILON) * weights

def rotate_half(values):
    middle = values.shape[-1] // 2
    return jnp.concatenate([-values[..., middle:], values[..., :middle]], axis=-1)

def layout_tables(length_row):
    places = jnp.arange(TOK_DEV, dtype=jnp.int32)
    ends = jnp.cumsum(length_row).astype(jnp.int32)
    passed = places[:, None] >= ends[None, :]
    segment = lax.optimization_barrier(jnp.sum(passed.astype(jnp.int32), axis=1))
    begins = lax.optimization_barrier(jnp.sum(jnp.where(passed, length_row[None, :], 0), axis=1)).astype(jnp.int32)
    position = (places - begins).astype(jnp.float32)
    frequency = THETA ** (-(jnp.arange(HEAD_DIM // 2, dtype=jnp.float32) * 2.0 / HEAD_DIM))
    angles = position[:, None] * frequency[None, :]
    cosine = jnp.concatenate([jnp.cos(angles), jnp.cos(angles)], axis=-1)
    sine = jnp.concatenate([jnp.sin(angles), jnp.sin(angles)], axis=-1)
    return (segment, cosine, sine)

def slot_layout(route_rows):
    flat_ids = route_rows.reshape(-1).astype(jnp.int32)
    count = flat_ids.shape[0]
    hits = (flat_ids[:, None] == jnp.arange(EXPERTS, dtype=jnp.int32)[None, :]).astype(jnp.int32)
    earlier = jnp.cumsum(hits, axis=0) - hits
    placed = lax.optimization_barrier(jnp.sum(earlier * hits, axis=1)).astype(jnp.int32)
    slot_of = flat_ids * CAP + placed
    source_row = jnp.arange(count, dtype=jnp.int32) // TOPK
    holder = jnp.zeros((EXPERTS * CAP,), jnp.int32).at[slot_of].set(source_row)
    filled = jnp.zeros((EXPERTS * CAP,), jnp.int32).at[slot_of].set(jnp.ones((count,), jnp.int32))
    return (slot_of, holder, filled)

def reference(tokens, routes, lengths, query_weight, key_weight, value_weight, output_weight, router_weight, first_gain, second_gain, expert_gate, expert_up, expert_down, cotangent):
    blocks = N_DP * N_EXPERT
    groups = HEADS // KV_HEADS
    scale = HEAD_DIM ** (-0.5)
    segment, cosine, sine = jax.vmap(layout_tables)(lengths)
    slot_of, holder, filled = jax.vmap(slot_layout)(routes.reshape(blocks, TOK_DEV, TOPK))
    choose = (routes[:, :, None] == jnp.arange(EXPERTS, dtype=jnp.int32)[None, None, :]).astype(jnp.float32)
    places = jnp.arange(TOK_DEV, dtype=jnp.int32)

    def rope(values, heads):
        shaped = values.reshape(blocks, TOK_DEV, heads, HEAD_DIM)
        return shaped * cosine[:, :, None, :] + rotate_half(shaped) * sine[:, :, None, :]

    def attend_block(inputs):
        queries, keys, values, seg_row = inputs
        grouped = queries.reshape(TOK_DEV, KV_HEADS, groups, HEAD_DIM)
        scores = low_back(jnp.einsum('qhgd,khd->hgqk', grouped, keys, precision=PRECISE))
        allowed = (seg_row[:, None] == seg_row[None, :]) & (places[None, :] <= places[:, None])
        scores = jnp.where(allowed[None, None], scores, -1e+30)
        highest = lax.optimization_barrier(jnp.max(scores, axis=-1, keepdims=True))
        raised = jnp.exp(scores - highest)
        probs = low(raised / lax.optimization_barrier(jnp.sum(raised, axis=-1, keepdims=True)))
        mixed = jnp.einsum('hgqk,khd->qhgd', probs, values, precision=PRECISE)
        return mixed.reshape(TOK_DEV, HEADS * HEAD_DIM)

    def forward(inputs, q_weight, k_weight, v_weight, o_weight, r_weight, gain_one, gain_two, gate_weight, up_weight, down_weight):
        normed_one = low(normalize(inputs, gain_one))
        q_lin = low_back(jnp.dot(normed_one, q_weight, precision=PRECISE))
        k_lin = low_back(jnp.dot(normed_one, k_weight, precision=PRECISE))
        v_lin = low_back(jnp.dot(normed_one, v_weight, precision=PRECISE))
        queries = low(rope(q_lin, HEADS) * scale)
        keys = low(rope(k_lin, KV_HEADS))
        values = low(v_lin).reshape(blocks, TOK_DEV, KV_HEADS, HEAD_DIM)
        mixed = lax.map(jax.checkpoint(attend_block), (queries, keys, values, segment))
        attended = low(low_back(mixed.reshape(TOKENS, HEADS * HEAD_DIM)))
        residual = inputs + low_back(jnp.dot(attended, o_weight, precision=PRECISE))
        normed_two = low(normalize(residual, gain_two))
        logits = low_back(jnp.dot(normed_two, r_weight, precision=PRECISE))
        chosen = lax.optimization_barrier(jnp.sum(choose * logits[:, None, :], axis=-1))
        highest = lax.optimization_barrier(jnp.max(chosen, axis=-1, keepdims=True))
        raised = jnp.exp(chosen - highest)
        gates = raised / lax.optimization_barrier(jnp.sum(raised, axis=-1, keepdims=True))

        def expert_block(pieces):
            normed, gate_rows, slot_row, holder_row, filled_row = pieces
            entering = low_back(normed[holder_row] * filled_row.astype(jnp.float32)[:, None]).reshape(EXPERTS, CAP, D)
            gate_pre = low_back(jnp.einsum('ecd,edf->ecf', entering, gate_weight, precision=PRECISE))
            up_pre = low_back(jnp.einsum('ecd,edf->ecf', entering, up_weight, precision=PRECISE))
            hidden = low(gate_pre * jax.nn.sigmoid(gate_pre) * up_pre)
            produced = jnp.einsum('ecf,efd->ecd', hidden, down_weight, precision=PRECISE)
            produced = low_back(low(produced)).reshape(EXPERTS * CAP, D)
            picked = produced[slot_row].reshape(TOK_DEV, TOPK, D)
            return lax.optimization_barrier(jnp.sum(gate_rows[:, :, None] * picked, axis=1))
        mixture = lax.map(jax.checkpoint(expert_block), (normed_two.reshape(blocks, TOK_DEV, D), gates.reshape(blocks, TOK_DEV, TOPK), slot_of, holder, filled))
        return residual + mixture.reshape(TOKENS, D)
    primals = (tokens.astype(jnp.float32), query_weight.astype(jnp.float32), key_weight.astype(jnp.float32), value_weight.astype(jnp.float32), output_weight.astype(jnp.float32), router_weight.astype(jnp.float32), first_gain.astype(jnp.float32), second_gain.astype(jnp.float32), expert_gate.astype(jnp.float32), expert_up.astype(jnp.float32), expert_down.astype(jnp.float32))
    result, pullback = jax.vjp(forward, *primals)
    grads = pullback(cotangent.astype(jnp.float32))
    return (result.astype(jnp.bfloat16), grads[0], grads[1], grads[2], grads[3], grads[4], grads[5], grads[6], grads[7], grads[8], grads[9], grads[10])
```

```python
import jax
import jax.numpy as jnp
from jax import lax
from jax.experimental import pallas as pl
from jax.experimental.pallas import tpu as pltpu
from jax.sharding import PartitionSpec as P

D = 1024
HEADS = 16
KV_HEADS = 8
HEAD_DIM = 64
EXPERTS = 32
TOPK = 8
CAP = 128
FF = 512
BLOCK = 256
EXTRA = 16
HELD = BLOCK + EXTRA
HD = HEADS * HEAD_DIM
KVD = KV_HEADS * HEAD_DIM

EPSILON = 1e-06
THETA = 10000.0
F32 = jnp.float32
BF16 = jnp.bfloat16

CORE, X_WAY, Y_WAY = 1, 2, 4


def layout_tables(length_row, count):
    places = jnp.arange(count, dtype=jnp.int32)
    ends = jnp.cumsum(length_row)
    passed = places[:, None] >= ends[None, :]
    begins = jnp.sum(jnp.where(passed, length_row[None, :], 0), axis=1)
    position = (places - begins).astype(F32)
    frequency = THETA ** (-(jnp.arange(HEAD_DIM // 2, dtype=F32) * 2.0 / HEAD_DIM))
    angles = position[:, None] * frequency[None, :]
    cosine = jnp.concatenate([jnp.cos(angles), jnp.cos(angles)], axis=-1)
    sine = jnp.concatenate([jnp.sin(angles), jnp.sin(angles)], axis=-1)
    return (cosine, sine)


def contract_rows(left, right):
    return lax.dot_general(left, right, (((0,), (0,)), ((), ())), preferred_element_type=F32)


def times_transpose(left, right):
    return lax.dot_general(left, right, (((1,), (1,)), ((), ())), preferred_element_type=F32)


def times(left, right):
    return jnp.dot(left, right, preferred_element_type=F32)


def rotate(values):
    width = values.shape[1]
    lane = lax.broadcasted_iota(jnp.int32, values.shape, 1)
    half = HEAD_DIM // 2
    return jnp.where(
        lax.rem(lane, HEAD_DIM) < half,
        -pltpu.roll(values, width - half, 1),
        pltpu.roll(values, half, 1),
    )


def wide(table, width):
    return jnp.concatenate([table] * (width // table.shape[1]), axis=1)


def allowed_pairs(length_ref, count):
    row = lax.broadcasted_iota(jnp.int32, (count, count), 0)
    column = lax.broadcasted_iota(jnp.int32, (count, count), 1)
    allowed = column <= row
    end = 0
    for s in range(length_ref.shape[0] - 1):
        end = end + length_ref[s]
        allowed = allowed & ((row >= end) == (column >= end))
    allowed = jnp.where(allowed, 1.0, 0.0)
    return jnp.concatenate([allowed, allowed], axis=0) > 0.0


def pair(value, h):
    at = 2 * HEAD_DIM * h
    return jnp.concatenate(
        [value[:, at : at + HEAD_DIM], value[:, at + HEAD_DIM : at + 2 * HEAD_DIM]], axis=0
    )


def beside(value):
    count = value.shape[0] // 2
    return jnp.concatenate([value[:count], value[count:]], axis=1)


def key_head(value, h):
    return value[:, HEAD_DIM * h : HEAD_DIM * (h + 1)]


def gains(dense_ref):
    lines = dense_ref[:, 3 * D :].astype(F32).T
    return lines[EXPERTS : EXPERTS + 1], lines[EXPERTS + 1 : EXPERTS + 2]


SCALE = HEAD_DIM ** (-0.5)
QKV = HD + 2 * KVD
WHOLE = pl.BlockSpec(memory_space=pltpu.VMEM)
SCALARS = pl.BlockSpec(memory_space=pltpu.SMEM)


def forward_call(lengths, tokens, dense, cosine, sine):
    count = tokens.shape[0]

    def body(
        length_ref, token_ref, dense_ref, cos_ref, sin_ref,
        n1_ref, q_ref, k_ref, v_ref, att_ref, lse_ref, res_ref, n2_ref, logit_ref,
    ):
        gain_a, gain_b = gains(dense_ref)
        x = token_ref[...].astype(F32)
        r1 = lax.rsqrt(jnp.mean(x * x, axis=1, keepdims=True) + EPSILON)
        n1 = (x * r1 * gain_a).astype(BF16)
        n1_ref[...] = n1
        qkv = times(n1, dense_ref[:, :QKV])
        q_lin, k_lin = qkv[:, :HD], qkv[:, HD : HD + KVD]
        cos, sin = wide(cos_ref[...], HD), wide(sin_ref[...], HD)
        q = ((q_lin * cos + rotate(q_lin) * sin) * SCALE).astype(BF16)
        k = (k_lin * cos[:, :KVD] + rotate(k_lin) * sin[:, :KVD]).astype(BF16)
        v = qkv[:, HD + KVD :].astype(BF16)
        q_ref[...], k_ref[...], v_ref[...] = q, k, v
        allowed = allowed_pairs(length_ref, count)
        lane = lax.broadcasted_iota(jnp.int32, (count, 128), 1)
        lse = jnp.zeros((count, 128), F32)
        for h in range(KV_HEADS):
            scores = times_transpose(pair(q, h), key_head(k, h))
            scores = jnp.where(allowed, scores, -1e30)
            highest = jnp.max(scores, axis=1, keepdims=True)
            raised = jnp.exp(scores - highest)
            total = jnp.sum(raised, axis=1, keepdims=True)
            probs = (raised / total).astype(BF16)
            mixed = times(probs, key_head(v, h))
            att_ref[:, 2 * HEAD_DIM * h : 2 * HEAD_DIM * (h + 1)] = beside(mixed).astype(BF16)
            logs = highest + jnp.log(total)
            lse = jnp.where(lane == 2 * h, logs[:count], lse)
            lse = jnp.where(lane == 2 * h + 1, logs[count:], lse)
        lse_ref[...] = lse
        residual = x + times(att_ref[...], dense_ref[:, QKV : QKV + D])
        res_ref[...] = residual
        r2 = lax.rsqrt(jnp.mean(residual * residual, axis=1, keepdims=True) + EPSILON)
        n2 = (residual * r2 * gain_b).astype(BF16)
        n2_ref[...] = n2
        logit_ref[...] = times(n2, dense_ref[:, 3 * D :])

    def out(width, dtype):
        return jax.ShapeDtypeStruct((count, width), dtype)

    return pl.pallas_call(
        body,
        in_specs=[SCALARS] + [WHOLE] * 4,
        out_specs=[WHOLE] * 9,
        out_shape=[
            out(D, BF16), out(HD, BF16), out(KVD, BF16), out(KVD, BF16), out(HD, BF16),
            out(128, F32), out(D, F32), out(D, BF16), out(128, F32),
        ],
        compiler_params=pltpu.CompilerParams(vmem_limit_bytes=56 * 1024 * 1024),
        cost_estimate=pl.CostEstimate(flops=50 * 10**9, bytes_accessed=10**7, transcendentals=0),
        name="attention_forward",
    )(lengths, tokens, dense, cosine, sine)


def backward_call(lengths, tokens, cotangent, dense, cosine, sine, kept, logit_back, back_rows):
    count = tokens.shape[0]

    def body(
        length_ref, token_ref, dy_ref, dense_ref, cos_ref, sin_ref,
        n1_ref, q_ref, k_ref, v_ref, att_ref, lse_ref, res_ref, n2_ref, lb_ref, back_ref,
        input_ref, late_ref, early_ref,
    ):
        gain_a, gain_b = gains(dense_ref)
        residual = res_ref[...]
        r2 = lax.rsqrt(jnp.mean(residual * residual, axis=1, keepdims=True) + EPSILON)
        back = times_transpose(lb_ref[...], dense_ref[:, 3 * D :]) + back_ref[...]
        second_terms = (back * residual * r2).astype(BF16)
        scaled = back * gain_b
        residual_back = (
            dy_ref[...].astype(F32)
            + r2 * scaled
            - residual * (r2 * r2 * r2) * jnp.mean(scaled * residual, axis=1, keepdims=True)
        )
        branch_back = residual_back.astype(BF16)
        early_ref[...] = contract_rows(att_ref[...], branch_back).astype(BF16)
        att_back = times_transpose(branch_back, dense_ref[:, QKV : QKV + D]).astype(BF16)
        q, k, v, lse = q_ref[...], k_ref[...], v_ref[...], lse_ref[...]
        allowed = allowed_pairs(length_ref, count)
        q_back, k_back, v_back = [], [], []
        for h in range(KV_HEADS):
            queries, keys, values = pair(q, h), key_head(k, h), key_head(v, h)
            grads = pair(att_back, h)
            logs = jnp.concatenate([lse[:, 2 * h : 2 * h + 1], lse[:, 2 * h + 1 : 2 * h + 2]], axis=0)
            scores = jnp.where(allowed, times_transpose(queries, keys), -1e30)
            probs = jnp.exp(scores - logs)
            prob_back = times_transpose(grads, values)
            spread = jnp.sum(prob_back * probs, axis=1, keepdims=True)
            score_back = (probs * (prob_back - spread)).astype(BF16)
            q_back.append(beside(times(score_back, keys)))
            k_back.append(contract_rows(score_back, queries))
            v_back.append(contract_rows(probs.astype(BF16), grads))
        q_back = jnp.concatenate(q_back, axis=1)
        k_back = jnp.concatenate(k_back, axis=1)
        v_back = jnp.concatenate(v_back, axis=1)
        cos, sin = wide(cos_ref[...], HD), wide(sin_ref[...], HD)
        q_back = ((q_back * cos - rotate(q_back * sin)) * SCALE).astype(BF16)
        k_back = (k_back * cos[:, :KVD] - rotate(k_back * sin[:, :KVD])).astype(BF16)
        qkv_back = jnp.concatenate([q_back, k_back, v_back.astype(BF16)], axis=1)
        late_ref[:, :QKV] = contract_rows(n1_ref[...], qkv_back).astype(BF16)
        first_back = times_transpose(qkv_back, dense_ref[:, :QKV])
        x = token_ref[...].astype(F32)
        r1 = lax.rsqrt(jnp.mean(x * x, axis=1, keepdims=True) + EPSILON)
        first_terms = (first_back * x * r1).astype(BF16)
        scaled = first_back * gain_a
        input_ref[...] = (
            residual_back
            + r1 * scaled
            - x * (r1 * r1 * r1) * jnp.mean(scaled * x, axis=1, keepdims=True)
        )
        lane = lax.broadcasted_iota(jnp.int32, (count, 128), 1)
        marks = [jnp.where(lane == EXPERTS + s, 1.0, 0.0).astype(BF16) for s in (0, 1)]
        late_ref[:, QKV:] = (
            contract_rows(n2_ref[...], lb_ref[...])
            + contract_rows(first_terms, marks[0])
            + contract_rows(second_terms, marks[1])
        ).astype(BF16)

    return pl.pallas_call(
        body,
        in_specs=[SCALARS] + [WHOLE] * 15,
        out_specs=[WHOLE] * 3,
        out_shape=[
            jax.ShapeDtypeStruct((count, D), F32),
            jax.ShapeDtypeStruct((D, QKV + 128), BF16),
            jax.ShapeDtypeStruct((D, D), BF16),
        ],
        compiler_params=pltpu.CompilerParams(vmem_limit_bytes=56 * 1024 * 1024),
        cost_estimate=pl.CostEstimate(flops=50 * 10**9, bytes_accessed=10**7, transcendentals=0),
        name="attention_backward",
    )(lengths, tokens, cotangent, dense, cosine, sine, *kept[:8], logit_back, back_rows)


def swap(value, axis, mask):
    size = lax.axis_size(axis)
    return lax.ppermute(value, axis, [(k, k ^ mask) for k in range(size)])


def tie(value, *first):
    return lax.optimization_barrier((value, first))[0]


def pack_weights(gate, up, down):
    rows = gate.shape[1]
    parts = [down[:, at : at + rows] for at in range(0, FF, rows)]
    return jnp.concatenate([gate, up] + parts, axis=2)


def expert_call(expert, rows, grads, weights, shards, before):
    steps = rows[0].shape[0] // HELD
    chained = before is not None
    size = D // shards
    squares = [(s, q) for s in range(shards) for q in range(FF // size)]

    def body(expert_ref, *refs):
        row_refs, grad_refs, weight_ref = refs[0:4], refs[4:8], refs[8]
        at = 9
        if chained:
            mix_before, back_before = refs[9:13], refs[13:17]
            at = 17
        mix_refs, back_refs = refs[at : at + 4], refs[at + 4 : at + 8]
        weight_grad_ref, down, gu_total, down_total = refs[at + 8 :]
        step = pl.program_id(0)

        @pl.when(step == 0)
        def _():
            gu_total[...] = jnp.zeros_like(gu_total)
            down_total[...] = jnp.zeros_like(down_total)
            for s, q in squares:
                down[q * size : (q + 1) * size, s * size : (s + 1) * size] = weight_ref[
                    s * size : (s + 1) * size, 2 * FF + q * size : 2 * FF + (q + 1) * size
                ]

        def by_token(value):
            value = value[0:1] + value[1:2]
            return sum(value[:, at : at + BLOCK] for at in range(0, D, BLOCK))

        counts, gate_lines = [], []
        for b in range(4):
            named = grad_refs[b][BLOCK:, :].astype(F32)[0:2] == expert_ref[0].astype(F32)
            gates = row_refs[b][BLOCK:, :].astype(F32)
            gates = gates[0:2] + gates[2:4]
            counts.append(by_token(jnp.where(named, 1.0, 0.0)))
            gate_lines.append(by_token(jnp.where(named, gates, 0.0)))
        hit = jnp.concatenate(counts + [jnp.zeros((4, BLOCK), F32)], axis=0)
        earlier = lax.broadcasted_iota(jnp.int32, (BLOCK, BLOCK), 0) < lax.broadcasted_iota(
            jnp.int32, (BLOCK, BLOCK), 1
        )
        slots = times(hit.astype(BF16), jnp.where(earlier, 1.0, 0.0).astype(BF16))
        slots = jnp.where(hit > 0.0, slots, -1.0).astype(jnp.int32)
        slot_ids = lax.broadcasted_iota(jnp.int32, (CAP, BLOCK), 0)
        hots, hots_low, z, raw, gate_cols = [], [], [], [], []
        for b in range(4):
            hot = slots[b : b + 1] == slot_ids
            hot_low = jnp.where(hot, 1.0, 0.0).astype(BF16)
            z.append(times(hot_low, row_refs[b][:BLOCK, :]).astype(BF16))
            raw.append(times(hot_low, grad_refs[b][:BLOCK, :]))
            gate_cols.append(
                jnp.sum(jnp.where(hot, gate_lines[b], 0.0), axis=1, keepdims=True)
            )
            hots.append(hot)
            hots_low.append(hot_low)
        z = jnp.concatenate(z, axis=0)
        raw = jnp.concatenate(raw, axis=0)
        gate_col = jnp.concatenate(gate_cols, axis=0)
        both = times(z, weight_ref[:, : 2 * FF])
        gate_pre, up_pre = both[:, :FF], both[:, FF:]
        sigma = jax.nn.sigmoid(gate_pre)
        activated = gate_pre * sigma
        hidden = (activated * up_pre).astype(BF16)
        produced = times(hidden, down[...]).astype(BF16).astype(F32)
        gate_back = jnp.sum(raw * produced, axis=1, keepdims=True)
        weighted = (gate_col * produced).astype(BF16)
        slot_back = (gate_col * raw).astype(BF16)
        hidden_back = times_transpose(slot_back, down[...])
        gate_slope = (hidden_back * up_pre * sigma * (1.0 + gate_pre * (1.0 - sigma))).astype(BF16)
        up_slope = (hidden_back * activated).astype(BF16)
        slopes = jnp.concatenate([gate_slope, up_slope], axis=1)
        gu_total[...] += contract_rows(z, slopes)
        down_total[...] += contract_rows(hidden, slot_back)
        entry_back = times_transpose(slopes, weight_ref[:, : 2 * FF]).astype(BF16)
        ranks = lax.broadcasted_iota(jnp.int32, (EXPERTS // 4, BLOCK), 0)
        for b in range(4):
            part = slice(b * CAP, (b + 1) * CAP)
            mixed = contract_rows(hots_low[b], weighted[part])
            back = contract_rows(hots_low[b], entry_back[part])
            line = jnp.sum(jnp.where(hots[b], gate_back[part], 0.0), axis=0, keepdims=True)
            extra = jnp.concatenate(
                [jnp.where(ranks * 4 + q == expert_ref[0], line, 0.0) for q in range(4)], axis=1
            )
            high = extra.astype(BF16).astype(F32)
            extra = jnp.concatenate([high, extra - high], axis=0)
            if chained:
                mixed = mixed + mix_before[b][:BLOCK, :].astype(F32)
                back = back + back_before[b][:BLOCK, :].astype(F32)
                extra = extra + back_before[b][BLOCK:, :].astype(F32)
            mix_refs[b][:BLOCK, :] = mixed.astype(BF16)
            mix_refs[b][BLOCK:, :] = jnp.zeros((EXTRA, D), BF16)
            back_refs[b][:BLOCK, :] = back.astype(BF16)
            back_refs[b][BLOCK:, :] = extra.astype(BF16)

        @pl.when(step == steps - 1)
        def _():
            weight_grad_ref[:, : 2 * FF] = gu_total[...].astype(BF16)
            for s, q in squares:
                weight_grad_ref[
                    s * size : (s + 1) * size, 2 * FF + q * size : 2 * FF + (q + 1) * size
                ] = down_total[q * size : (q + 1) * size, s * size : (s + 1) * size].astype(BF16)

    row_spec = pl.BlockSpec((HELD, D), lambda s: (s, 0))
    weight_spec = pl.BlockSpec((D, 3 * FF), lambda s: (0, 0), pipeline_mode=pl.Buffered(1))
    rows_shape = jax.ShapeDtypeStruct(rows[0].shape, BF16)
    extra = list(before[0]) + list(before[1]) if chained else []
    outs = pl.pallas_call(
        body,
        grid=(steps,),
        in_specs=[pl.BlockSpec(memory_space=pltpu.SMEM)]
        + [row_spec] * 8
        + [weight_spec]
        + [row_spec] * len(extra),
        out_specs=[row_spec] * 8 + [weight_spec],
        out_shape=[rows_shape] * 8
        + [jax.ShapeDtypeStruct((D, 3 * FF), BF16)],
        scratch_shapes=[
            pltpu.VMEM((FF, D), BF16),
            pltpu.VMEM((D, 2 * FF), F32),
            pltpu.VMEM((FF, D), F32),
        ],
        compiler_params=pltpu.CompilerParams(vmem_limit_bytes=60 * 1024 * 1024),
        cost_estimate=pl.CostEstimate(flops=1000, bytes_accessed=1000, transcendentals=0),
        name="experts",
    )(expert, *rows, *grads, weights, *extra)
    return outs[0:4], outs[4:8], outs[8]


def with_extra(block, low):
    count = TOPK * BLOCK // D
    lines = [part.reshape(count, D).astype(BF16) for part in low]
    lines.append(jnp.zeros((EXTRA - count * len(low), D), BF16))
    return jnp.concatenate([block] + lines, axis=0)


class Cube:
    HALF = 144

    def __init__(self, experts_here):
        self.place = lax.axis_index("expert")
        self.line = lax.axis_index("dp")
        self.odd = lax.rem(self.line, 2)
        self.share = experts_here // 2
        self.shards = 4
        self.own_ids = experts_here * self.place + self.share * self.odd + jnp.arange(self.share)

    def spread(self, block):
        first, second = block[: self.HALF], block[self.HALF :]
        first_x = swap(first, "expert", X_WAY)
        second_y = swap(second, "expert", Y_WAY)
        first_y = swap(jnp.concatenate([first, first_x]), "expert", Y_WAY)
        second_x = swap(jnp.concatenate([second, second_y]), "expert", X_WAY)
        return first, second, first_x, second_x, first_y, second_y

    def join(self, pieces):
        first, second, first_x, second_x, first_y, second_y = pieces
        rest = HELD - self.HALF
        return jnp.concatenate(
            [
                first,
                second,
                first_x,
                second_x[:rest],
                first_y[: self.HALF],
                second_y,
                first_y[self.HALF :],
                second_x[rest:],
            ],
            axis=0,
        )

    def cross(self, block):
        return swap(block, "dp", 1)

    def both_cores(self, near, far):
        near, far = self.join(near), self.join(far)
        return [near, swap(near, "expert", CORE), far, swap(far, "expert", CORE)]


    def fold_cores(self, parts):
        near, near_other, far, far_other = parts
        far = (far.astype(F32) + swap(far_other, "expert", CORE).astype(F32)).astype(BF16)
        near = (near.astype(F32) + swap(near_other, "expert", CORE).astype(F32)).astype(BF16)
        return far, near

    def fold_once(self, parts):
        folded = []
        for part in parts:
            part = part.reshape(2, 2, HELD, D)
            first, second = part[:, :, : self.HALF], part[:, :, self.HALF :]
            first = first[0].astype(F32) + swap(first[1], "expert", Y_WAY).astype(F32)
            second = second[:, 0].astype(F32) + swap(second[:, 1], "expert", X_WAY).astype(F32)
            folded.append((first.astype(BF16), second.astype(BF16)))
        return folded

    def fold_twice(self, folded):
        blocks = []
        for first, second in folded:
            first = first[0].astype(F32) + swap(first[1], "expert", X_WAY).astype(F32)
            second = second[0].astype(F32) + swap(second[1], "expert", Y_WAY).astype(F32)
            blocks.append(jnp.concatenate([first, second], axis=0).astype(BF16))
        return blocks

    def fold_planes(self, blocks):
        far, near = blocks
        return near.astype(F32) + swap(far, "dp", 1).astype(F32)

    def weight(self, shards, e):
        low, high = shards[e], shards[self.share + e]
        sent = jnp.stack([low, high, low, high])
        whole = lax.all_to_all(sent, "dp", split_axis=0, concat_axis=0, tiled=True)
        return whole.reshape(D, 3 * FF)

    def weight_grad(self, total):
        parts = total.reshape(4, D // 4, 3 * FF)
        return lax.all_to_all(parts, "dp", split_axis=0, concat_axis=0, tiled=True)

    def weight_grads(self, arrived):
        low = [got[0].astype(F32) + got[2].astype(F32) for got in arrived]
        high = [got[1].astype(F32) + got[3].astype(F32) for got in arrived]
        return jnp.stack(low + high)

    def gather_dense(self, shard):
        part, width = shard.shape[0] // 8, shard.shape[1]
        middle = width // 256 * 128
        own = lax.dynamic_slice_in_dim(shard, self.place * part, part, 0)[None, None]
        lines = jnp.zeros((4, 1, part, width), shard.dtype)
        for mask in range(4):
            piece = swap(own, "dp", mask) if mask else own
            lines = lax.dynamic_update_slice(lines, piece, (self.line ^ mask, 0, 0, 0))
        first, second = lines[..., :middle], lines[..., middle:]
        first_x = swap(first, "expert", X_WAY)
        second_y = swap(second, "expert", Y_WAY)
        firsts = swap(jnp.concatenate([first, first_x], axis=1), "expert", Y_WAY)
        seconds = swap(jnp.concatenate([second, second_y], axis=1), "expert", X_WAY)
        found = (
            (lines, 0, 0, (0,)),
            (first_x, X_WAY, 0, (0,)),
            (second_y, Y_WAY, middle, (0,)),
            (firsts, Y_WAY, 0, (0, X_WAY)),
            (seconds, X_WAY, middle, (0, Y_WAY)),
        )
        whole = jnp.zeros((4, 8, part, width), shard.dtype)
        for pieces, mask, at, more in found:
            other = swap(pieces, "expert", CORE)
            for k, bits in enumerate(more):
                where = self.place ^ (mask | bits)
                whole = lax.dynamic_update_slice(whole, pieces[:, k : k + 1], (0, where, 0, at))
                where = where ^ CORE
                whole = lax.dynamic_update_slice(whole, other[:, k : k + 1], (0, where, 0, at))
        return whole.reshape(-1, width), lines


    def fold_dense(self, totals):
        core, x, y = [lax.rem(lax.div(self.place, way), 2) for way in (CORE, X_WAY, Y_WAY)]

        def fold(value, bit, axis, mask):
            kept = lax.dynamic_index_in_dim(value, bit, axis, keepdims=False)
            sent = lax.dynamic_index_in_dim(value, 1 - bit, axis, keepdims=False)
            return (kept.astype(F32) + swap(sent, "expert", mask).astype(F32)).astype(BF16)

        found = []
        for total, x_first in zip(totals, (False, True)):
            width, part = total.shape[1], total.shape[0] // 32
            lines = fold(total.reshape(4, 2, 2, 2, part, width), core, 3, CORE)
            if x_first:
                found.append(fold(fold(lines, x, 2, X_WAY), y, 1, Y_WAY))
            else:
                found.append(fold(fold(lines, y, 1, Y_WAY), x, 1, X_WAY))
        return found

    def sum_dense(self, found):
        sums = []
        for lines in found:
            summed = lax.dynamic_index_in_dim(lines, self.line, 0).astype(F32)
            for mask in (1, 2, 3):
                sent = lax.dynamic_index_in_dim(lines, self.line ^ mask, 0)
                summed = summed + swap(sent, "dp", mask).astype(F32)
            sums.append(summed.astype(BF16))
        return sums

    def spread_dense(self, sums):
        found = []
        for summed in sums:
            _, part, width = summed.shape
            whole = jnp.zeros((8, part, width), BF16)
            for mask in range(8):
                piece = swap(summed, "expert", mask) if mask else summed
                whole = lax.dynamic_update_slice(whole, piece, (self.place ^ mask, 0, 0))
            found.append(whole.reshape(-1, width).astype(F32))
        return found


class Plain:
    def __init__(self, experts_here):
        self.share = experts_here
        self.shards = lax.axis_size("dp")
        self.own_ids = experts_here * lax.axis_index("expert") + jnp.arange(experts_here)

    def spread(self, block):
        return block

    def cross(self, block):
        return block

    def both_cores(self, near, far):
        whole = lax.all_gather(near, "expert", axis=0, tiled=True)
        return jnp.split(whole, 4, axis=0)

    def fold_cores(self, parts):
        whole = jnp.concatenate(parts, axis=0)
        return [lax.psum_scatter(whole, "expert", scatter_dimension=0, tiled=True)]

    def fold_once(self, parts):
        return parts

    def fold_twice(self, parts):
        return parts

    def fold_planes(self, blocks):
        return blocks[0].astype(F32)

    def gather_dense(self, shard):
        part = shard.shape[0] // lax.axis_size("expert")
        own = lax.dynamic_slice_in_dim(shard, lax.axis_index("expert") * part, part, 0)
        return lax.all_gather(own, ("dp", "expert"), axis=0, tiled=True), own

    def weight(self, shards, e):
        return lax.all_gather(shards[e], "dp", axis=0, tiled=True)

    def weight_grad(self, total):
        return lax.psum_scatter(total, "dp", scatter_dimension=0, tiled=True)

    def weight_grads(self, arrived):
        return jnp.stack(arrived).astype(F32)

    def fold_dense(self, totals):
        both = ("dp", "expert")
        return [lax.psum_scatter(t, both, scatter_dimension=0, tiled=True) for t in totals]

    def sum_dense(self, sums):
        return sums

    def spread_dense(self, sums):
        return [lax.all_gather(t, "expert", axis=0, tiled=True).astype(F32) for t in sums]


def on_device(
    tokens,
    routes,
    lengths,
    query_weight,
    key_weight,
    value_weight,
    output_weight,
    router_weight,
    first_gain,
    second_gain,
    expert_gate,
    expert_up,
    expert_down,
    cotangent,
):
    tok_count = tokens.shape[0]
    here = expert_gate.shape[0]
    cube = lax.axis_size("dp") == 4 and lax.axis_size("expert") == 8 and here % 2 == 0
    plan = Cube(here) if cube else Plain(here)

    small = jnp.concatenate(
        [
            router_weight,
            first_gain[:, None],
            second_gain[:, None],
            jnp.zeros((router_weight.shape[0], 128 - EXPERTS - 2), BF16),
        ],
        axis=1,
    )
    grad_block = with_extra(cotangent, [routes.T.astype(F32)])
    grad_near = plan.spread(grad_block)
    dense, lines = plan.gather_dense(
        jnp.concatenate([query_weight, key_weight, value_weight, output_weight, small], axis=1)
    )
    grad_across = plan.cross(tie(grad_block, lines))
    grad_far = plan.spread(tie(grad_across, dense))
    shards = pack_weights(expert_gate, expert_up, expert_down)
    weights = [plan.weight(tie(shards, grad_across), 0)]

    cosine, sine = layout_tables(lengths[0], tok_count)
    cosine, sine = jnp.concatenate([cosine, cosine], axis=1), jnp.concatenate([sine, sine], axis=1)
    kept = forward_call(lengths[0], tokens, dense, cosine, sine)
    residual, normed_two, logits = kept[6:]
    logits = logits[:, :EXPERTS]
    choose = (routes[:, :, None] == jnp.arange(EXPERTS, dtype=jnp.int32)[None, None, :]).astype(F32)
    chosen = jnp.sum(choose * logits[:, None, :], axis=-1)
    top_chosen = jnp.max(chosen, axis=-1, keepdims=True)
    raised_gates = jnp.exp(chosen - top_chosen)
    gates = raised_gates / jnp.sum(raised_gates, axis=-1, keepdims=True)

    gate_lines = gates.T
    gate_high = lax.optimization_barrier(gate_lines.astype(BF16))
    gate_low = gate_lines - gate_high.astype(F32)
    block, grad_far = lax.optimization_barrier(
        (with_extra(normed_two, [gate_high, gate_low]), grad_far)
    )
    rows_across = plan.cross(block)
    rows = plan.both_cores(plan.spread(block), plan.spread(rows_across))
    grad_rows = plan.both_cores(grad_near, grad_far)
    for e in range(1, plan.share):
        weights.append(plan.weight(tie(shards, rows_across, weights[-1]), e))

    done, weight_parts = None, []
    for e in range(plan.share):
        mixes, backs, weight_part = expert_call(
            plan.own_ids[e : e + 1].astype(jnp.int32),
            rows,
            grad_rows,
            weights[e],
            plan.shards,
            done,
        )
        done = (mixes, backs)
        weight_parts.append(weight_part)

    arrived = [plan.weight_grad(weight_parts[0])]
    folded = plan.fold_once(plan.fold_cores(done[1]))
    mixes = plan.fold_once(plan.fold_cores(done[0]))
    folded, mixes, arrived = lax.optimization_barrier((folded, mixes, arrived))
    back_held = plan.fold_planes(plan.fold_twice(folded))
    back_rows = back_held[:BLOCK]
    owners_back = back_held[BLOCK : BLOCK + EXTRA // 2] + back_held[BLOCK + EXTRA // 2 :]
    owners_back = owners_back.reshape(EXPERTS, BLOCK)
    for part in weight_parts[1:]:
        arrived.append(plan.weight_grad(tie(part, back_rows)))
    mixes = plan.fold_twice(tie(mixes, back_rows))

    gate_back = jnp.sum(choose * owners_back.T[:, None, :], axis=-1)
    chosen_back = gates * (gate_back - jnp.sum(gates * gate_back, axis=-1, keepdims=True))
    logit_back = jnp.sum(chosen_back[:, :, None] * choose, axis=1).astype(BF16)
    logit_back = jnp.pad(logit_back, ((0, 0), (0, 128 - EXPERTS)))
    input_grad, late, early = backward_call(
        lengths[0], tokens, cotangent, dense, cosine, sine, kept, logit_back, back_rows
    )
    late, early, mixes = lax.optimization_barrier((late, early, mixes))
    sums, arrived = lax.optimization_barrier((plan.fold_dense([late, early]), arrived))
    mixture = plan.fold_planes(tie(mixes, sums))
    output = (residual + mixture[:BLOCK]).astype(BF16)
    late, early = plan.spread_dense(plan.sum_dense(sums))
    weight_grad = plan.weight_grads(arrived)
    return (
        output,
        input_grad,
        late[:, :HD],
        late[:, HD : HD + KVD],
        late[:, HD + KVD : HD + 2 * KVD],
        early,
        late[:, HD + 2 * KVD : HD + 2 * KVD + EXPERTS],
        late[:, HD + 2 * KVD + EXPERTS],
        late[:, HD + 2 * KVD + EXPERTS + 1],
        weight_grad[:, :, :FF],
        weight_grad[:, :, FF : 2 * FF],
        jnp.concatenate(
            jnp.split(weight_grad[:, :, 2 * FF :], FF // weight_grad.shape[1], axis=2), axis=1
        ),
    )


def solution(mesh):
    return jax.shard_map(
        on_device,
        mesh=mesh,
        in_specs=(
            P(("dp", "expert"), None),
            P(("dp", "expert"), None),
            P(("dp", "expert"), None),
            P("dp", None),
            P("dp", None),
            P("dp", None),
            P("dp", None),
            P("dp", None),
            P("dp"),
            P("dp"),
            P("expert", "dp", None),
            P("expert", "dp", None),
            P("expert", None, "dp"),
            P(("dp", "expert"), None),
        ),
        out_specs=(
            P(("dp", "expert"), None),
            P(("dp", "expert"), None),
            P("dp", None),
            P("dp", None),
            P("dp", None),
            P("dp", None),
            P("dp", None),
            P("dp"),
            P("dp"),
            P("expert", "dp", None),
            P("expert", "dp", None),
            P("expert", None, "dp"),
        ),
        check_vma=False,
    )
```

```python
import jax
import jax.numpy as jnp
from jax import lax
from jax.experimental import pallas as pl
from jax.experimental.pallas import tpu as pltpu
from jax.sharding import PartitionSpec as P

D = 1024
HEADS = 16
KV_HEADS = 8
HEAD_DIM = 64
EXPERTS = 32
TOPK = 8
CAP = 128
FF = 512
BLOCK = 256
EXTRA = 16
HELD = BLOCK + EXTRA
HALF = BLOCK // 2
HD = HEADS * HEAD_DIM
KVD = KV_HEADS * HEAD_DIM

EPSILON = 1e-06
THETA = 10000.0
F32 = jnp.float32
BF16 = jnp.bfloat16

CORE, X_WAY, Y_WAY = 1, 2, 4


def layout_tables(length_row, count):
    places = jnp.arange(count, dtype=jnp.int32)
    ends = jnp.cumsum(length_row)
    passed = places[:, None] >= ends[None, :]
    begins = jnp.sum(jnp.where(passed, length_row[None, :], 0), axis=1)
    position = (places - begins).astype(F32)
    frequency = THETA ** (-(jnp.arange(HEAD_DIM // 2, dtype=F32) * 2.0 / HEAD_DIM))
    angles = position[:, None] * frequency[None, :]
    cosine = jnp.concatenate([jnp.cos(angles), jnp.cos(angles)], axis=-1)
    sine = jnp.concatenate([jnp.sin(angles), jnp.sin(angles)], axis=-1)
    return (cosine, sine)


def contract_rows(left, right):
    return lax.dot_general(left, right, (((0,), (0,)), ((), ())), preferred_element_type=F32)


def times_transpose(left, right):
    return lax.dot_general(left, right, (((1,), (1,)), ((), ())), preferred_element_type=F32)


def times(left, right):
    return jnp.dot(left, right, preferred_element_type=F32)


def rotate(values):
    width = values.shape[1]
    lane = lax.broadcasted_iota(jnp.int32, values.shape, 1)
    half = HEAD_DIM // 2
    return jnp.where(
        lax.rem(lane, HEAD_DIM) < half,
        -pltpu.roll(values, width - half, 1),
        pltpu.roll(values, half, 1),
    )


def wide(table, width):
    return jnp.concatenate([table] * (width // table.shape[1]), axis=1)


def allowed_pairs(length_ref, count):
    row = lax.broadcasted_iota(jnp.int32, (count, count), 0)
    column = lax.broadcasted_iota(jnp.int32, (count, count), 1)
    allowed = column <= row
    end = 0
    for s in range(length_ref.shape[0] - 1):
        end = end + length_ref[s]
        allowed = allowed & ((row >= end) == (column >= end))
    allowed = jnp.where(allowed, 1.0, 0.0)
    return jnp.concatenate([allowed, allowed], axis=0) > 0.0


def pair(value, h):
    at = 2 * HEAD_DIM * h
    return jnp.concatenate(
        [value[:, at : at + HEAD_DIM], value[:, at + HEAD_DIM : at + 2 * HEAD_DIM]], axis=0
    )


def beside(value):
    count = value.shape[0] // 2
    return jnp.concatenate([value[:count], value[count:]], axis=1)


def key_head(value, h):
    return value[:, HEAD_DIM * h : HEAD_DIM * (h + 1)]


def gains(dense_ref):
    lines = dense_ref[:, 3 * D :].astype(F32).T
    return lines[EXPERTS : EXPERTS + 1], lines[EXPERTS + 1 : EXPERTS + 2]


SCALE = HEAD_DIM ** (-0.5)
QKV = HD + 2 * KVD
WHOLE = pl.BlockSpec(memory_space=pltpu.VMEM)
SCALARS = pl.BlockSpec(memory_space=pltpu.SMEM)


def forward_call(lengths, tokens, parts, cosine, sine):
    count = tokens.shape[0]
    columns = [at for _, at, _ in parts]
    starts = jnp.concatenate([start for _, _, start in parts]).astype(jnp.int32)
    parts = [part for part, _, _ in parts]

    def body(length_ref, start_ref, token_ref, cos_ref, sin_ref, *refs):
        part_refs, outs = refs[: len(parts)], refs[len(parts) :]
        n1_ref, q_ref, k_ref, v_ref, att_ref, lse_ref, res_ref, n2_ref, logit_ref, dense_ref = outs
        for p, part_ref in enumerate(part_refs):
            pieces, rows, width = part_ref.shape
            for s in range(pieces):
                start = pl.multiple_of(start_ref[p * pieces + s], rows)
                dense_ref[pl.ds(start, rows), columns[p] : columns[p] + width] = part_ref[s]
        gain_a, gain_b = gains(dense_ref)
        x = token_ref[...].astype(F32)
        r1 = lax.rsqrt(jnp.mean(x * x, axis=1, keepdims=True) + EPSILON)
        n1 = (x * r1 * gain_a).astype(BF16)
        n1_ref[...] = n1
        qkv = times(n1, dense_ref[:, :QKV])
        q_lin, k_lin = qkv[:, :HD], qkv[:, HD : HD + KVD]
        cos, sin = wide(cos_ref[...], HD), wide(sin_ref[...], HD)
        q = ((q_lin * cos + rotate(q_lin) * sin) * SCALE).astype(BF16)
        k = (k_lin * cos[:, :KVD] + rotate(k_lin) * sin[:, :KVD]).astype(BF16)
        v = qkv[:, HD + KVD :].astype(BF16)
        q_ref[...], k_ref[...], v_ref[...] = q, k, v
        allowed = allowed_pairs(length_ref, count)
        lane = lax.broadcasted_iota(jnp.int32, (count, 128), 1)
        lse = jnp.zeros((count, 128), F32)
        for h in range(KV_HEADS):
            scores = times_transpose(pair(q, h), key_head(k, h))
            scores = jnp.where(allowed, scores, -1e30)
            highest = jnp.max(scores, axis=1, keepdims=True)
            raised = jnp.exp(scores - highest)
            total = jnp.sum(raised, axis=1, keepdims=True)
            probs = (raised / total).astype(BF16)
            mixed = times(probs, key_head(v, h))
            att_ref[:, 2 * HEAD_DIM * h : 2 * HEAD_DIM * (h + 1)] = beside(mixed).astype(BF16)
            logs = highest + jnp.log(total)
            lse = jnp.where(lane == 2 * h, logs[:count], lse)
            lse = jnp.where(lane == 2 * h + 1, logs[count:], lse)
        lse_ref[...] = lse
        residual = x + times(att_ref[...], dense_ref[:, QKV : QKV + D])
        res_ref[...] = residual
        r2 = lax.rsqrt(jnp.mean(residual * residual, axis=1, keepdims=True) + EPSILON)
        n2 = (residual * r2 * gain_b).astype(BF16)
        n2_ref[...] = n2
        logit_ref[...] = times(n2, dense_ref[:, 3 * D :])

    def out(width, dtype):
        return jax.ShapeDtypeStruct((count, width), dtype)

    return pl.pallas_call(
        body,
        in_specs=[SCALARS] * 2 + [WHOLE] * (3 + len(parts)),
        out_specs=[WHOLE] * 10,
        out_shape=[
            out(D, BF16), out(HD, BF16), out(KVD, BF16), out(KVD, BF16), out(HD, BF16),
            out(128, F32), out(D, F32), out(D, BF16), out(128, F32),
            jax.ShapeDtypeStruct((D, 3 * D + 128), BF16),
        ],
        compiler_params=pltpu.CompilerParams(vmem_limit_bytes=56 * 1024 * 1024),
        cost_estimate=pl.CostEstimate(flops=1000, bytes_accessed=1000, transcendentals=0),
        name="attention_forward",
    )(lengths, starts, tokens, cosine, sine, *parts)


def backward_call(lengths, tokens, cotangent, dense, cosine, sine, kept, logit_back, back_rows):
    count = tokens.shape[0]

    def body(
        length_ref, token_ref, dy_ref, dense_ref, cos_ref, sin_ref,
        n1_ref, q_ref, k_ref, v_ref, att_ref, lse_ref, res_ref, n2_ref, lb_ref, back_ref,
        input_ref, late_ref, early_ref,
    ):
        gain_a, gain_b = gains(dense_ref)
        residual = res_ref[...]
        r2 = lax.rsqrt(jnp.mean(residual * residual, axis=1, keepdims=True) + EPSILON)
        back = times_transpose(lb_ref[...], dense_ref[:, 3 * D :]) + back_ref[...]
        second_terms = (back * residual * r2).astype(BF16)
        scaled = back * gain_b
        residual_back = (
            dy_ref[...].astype(F32)
            + r2 * scaled
            - residual * (r2 * r2 * r2) * jnp.mean(scaled * residual, axis=1, keepdims=True)
        )
        branch_back = residual_back.astype(BF16)
        early_ref[...] = contract_rows(att_ref[...], branch_back).astype(BF16)
        att_back = times_transpose(branch_back, dense_ref[:, QKV : QKV + D]).astype(BF16)
        q, k, v, lse = q_ref[...], k_ref[...], v_ref[...], lse_ref[...]
        allowed = allowed_pairs(length_ref, count)
        q_back, k_back, v_back = [], [], []
        for h in range(KV_HEADS):
            queries, keys, values = pair(q, h), key_head(k, h), key_head(v, h)
            grads = pair(att_back, h)
            logs = jnp.concatenate([lse[:, 2 * h : 2 * h + 1], lse[:, 2 * h + 1 : 2 * h + 2]], axis=0)
            scores = jnp.where(allowed, times_transpose(queries, keys), -1e30)
            probs = jnp.exp(scores - logs)
            prob_back = times_transpose(grads, values)
            spread = jnp.sum(prob_back * probs, axis=1, keepdims=True)
            score_back = (probs * (prob_back - spread)).astype(BF16)
            q_back.append(beside(times(score_back, keys)))
            k_back.append(contract_rows(score_back, queries))
            v_back.append(contract_rows(probs.astype(BF16), grads))
        q_back = jnp.concatenate(q_back, axis=1)
        k_back = jnp.concatenate(k_back, axis=1)
        v_back = jnp.concatenate(v_back, axis=1)
        cos, sin = wide(cos_ref[...], HD), wide(sin_ref[...], HD)
        q_back = ((q_back * cos - rotate(q_back * sin)) * SCALE).astype(BF16)
        k_back = (k_back * cos[:, :KVD] - rotate(k_back * sin[:, :KVD])).astype(BF16)
        qkv_back = jnp.concatenate([q_back, k_back, v_back.astype(BF16)], axis=1)
        late_ref[:, :QKV] = contract_rows(n1_ref[...], qkv_back).astype(BF16)
        first_back = times_transpose(qkv_back, dense_ref[:, :QKV])
        x = token_ref[...].astype(F32)
        r1 = lax.rsqrt(jnp.mean(x * x, axis=1, keepdims=True) + EPSILON)
        first_terms = (first_back * x * r1).astype(BF16)
        scaled = first_back * gain_a
        input_ref[...] = (
            residual_back
            + r1 * scaled
            - x * (r1 * r1 * r1) * jnp.mean(scaled * x, axis=1, keepdims=True)
        )
        lane = lax.broadcasted_iota(jnp.int32, (count, 128), 1)
        marks = [jnp.where(lane == EXPERTS + s, 1.0, 0.0).astype(BF16) for s in (0, 1)]
        late_ref[:, QKV:] = (
            contract_rows(n2_ref[...], lb_ref[...])
            + contract_rows(first_terms, marks[0])
            + contract_rows(second_terms, marks[1])
        ).astype(BF16)

    return pl.pallas_call(
        body,
        in_specs=[SCALARS] + [WHOLE] * 15,
        out_specs=[WHOLE] * 3,
        out_shape=[
            jax.ShapeDtypeStruct((count, D), F32),
            jax.ShapeDtypeStruct((D, QKV + 128), BF16),
            jax.ShapeDtypeStruct((D, D), BF16),
        ],
        compiler_params=pltpu.CompilerParams(vmem_limit_bytes=56 * 1024 * 1024),
        cost_estimate=pl.CostEstimate(flops=50 * 10**9, bytes_accessed=10**7, transcendentals=0),
        name="attention_backward",
    )(lengths, tokens, cotangent, dense, cosine, sine, *kept[:8], logit_back, back_rows)


def swap(value, axis, mask):
    size = lax.axis_size(axis)
    return lax.ppermute(value, axis, [(k, k ^ mask) for k in range(size)])


def tie(value, *first):
    return lax.optimization_barrier((value, first))[0]


def pack_weights(gate, up, down):
    rows = gate.shape[1]
    parts = [down[:, at : at + rows] for at in range(0, FF, rows)]
    return jnp.concatenate([gate, up] + parts, axis=2)


def expert_call(expert, rows, grads, weights, shards, turned, before):
    steps = rows[0][0].shape[0] // HALF
    chained = before is not None
    size = D // shards
    squares = [(s, q) for s in range(shards) for q in range(FF // size)]

    def body(expert_ref, *refs):
        def pairs(at):
            return [refs[at + 2 * b : at + 2 * b + 2] for b in range(4)]

        row_refs, grad_refs, weight_ref = pairs(0), pairs(8), refs[16]
        at = 17
        if chained:
            mix_before, back_before = pairs(17), pairs(25)
            at = 33
        mix_refs, back_refs = pairs(at), pairs(at + 8)
        weight_grad_ref, down, gu_total, down_total = refs[at + 16 :]

        def block_of(pair_refs):
            return jnp.concatenate([pair_refs[0][...], pair_refs[1][:HALF, :]], axis=0)
        step = pl.program_id(0)

        @pl.when(step == 0)
        def _():
            gu_total[...] = jnp.zeros_like(gu_total)
            down_total[...] = jnp.zeros_like(down_total)
            for s, q in squares:
                down[q * size : (q + 1) * size, s * size : (s + 1) * size] = weight_ref[
                    s * size : (s + 1) * size, 2 * FF + q * size : 2 * FF + (q + 1) * size
                ]

        def by_token(value):
            value = value[0:1] + value[1:2]
            return sum(value[:, at : at + BLOCK] for at in range(0, D, BLOCK))

        counts, gate_lines = [], []
        for b in range(4):
            named = grad_refs[b][1][HALF:, :].astype(F32)[0:2] == expert_ref[0].astype(F32)
            gates = row_refs[b][1][HALF:, :].astype(F32)
            gates = gates[0:2] + gates[2:4]
            counts.append(by_token(jnp.where(named, 1.0, 0.0)))
            gate_lines.append(by_token(jnp.where(named, gates, 0.0)))
        hit = jnp.concatenate(counts + [jnp.zeros((4, BLOCK), F32)], axis=0)
        earlier = lax.broadcasted_iota(jnp.int32, (BLOCK, BLOCK), 0) < lax.broadcasted_iota(
            jnp.int32, (BLOCK, BLOCK), 1
        )
        slots = times(hit.astype(BF16), jnp.where(earlier, 1.0, 0.0).astype(BF16))
        slots = jnp.where(hit > 0.0, slots, -1.0).astype(jnp.int32)
        slot_ids = lax.broadcasted_iota(jnp.int32, (CAP, BLOCK), 0)
        hots, hots_low, z, raw, gate_cols = [], [], [], [], []
        for b in range(4):
            hot = slots[b : b + 1] == slot_ids
            hot_low = jnp.where(hot, 1.0, 0.0).astype(BF16)
            z.append(times(hot_low, block_of(row_refs[b])).astype(BF16))
            raw.append(times(hot_low, block_of(grad_refs[b])))
            gate_cols.append(
                jnp.sum(jnp.where(hot, gate_lines[b], 0.0), axis=1, keepdims=True)
            )
            hots.append(hot)
            hots_low.append(hot_low)
        z = jnp.concatenate(z, axis=0)
        raw = jnp.concatenate(raw, axis=0)
        gate_col = jnp.concatenate(gate_cols, axis=0)
        both = times(z, weight_ref[:, : 2 * FF])
        gate_pre, up_pre = both[:, :FF], both[:, FF:]
        sigma = jax.nn.sigmoid(gate_pre)
        activated = gate_pre * sigma
        hidden = (activated * up_pre).astype(BF16)
        produced = times(hidden, down[...]).astype(BF16).astype(F32)
        gate_back = jnp.sum(raw * produced, axis=1, keepdims=True)
        weighted = (gate_col * produced).astype(BF16)
        slot_back = (gate_col * raw).astype(BF16)
        hidden_back = times_transpose(slot_back, down[...])
        gate_slope = (hidden_back * up_pre * sigma * (1.0 + gate_pre * (1.0 - sigma))).astype(BF16)
        up_slope = (hidden_back * activated).astype(BF16)
        slopes = jnp.concatenate([gate_slope, up_slope], axis=1)
        gu_total[...] += contract_rows(z, slopes)
        down_total[...] += contract_rows(hidden, slot_back)
        entry_back = times_transpose(slopes, weight_ref[:, : 2 * FF]).astype(BF16)
        ranks = lax.broadcasted_iota(jnp.int32, (EXPERTS // 4, BLOCK), 0)
        for b in range(4):
            part = slice(b * CAP, (b + 1) * CAP)
            mixed = contract_rows(hots_low[b], weighted[part])
            back = contract_rows(hots_low[b], entry_back[part])
            line = jnp.sum(jnp.where(hots[b], gate_back[part], 0.0), axis=0, keepdims=True)
            extra = jnp.concatenate(
                [jnp.where(ranks * 4 + q == expert_ref[0], line, 0.0) for q in range(4)], axis=1
            )
            high = extra.astype(BF16).astype(F32)
            extra = jnp.concatenate([high, extra - high], axis=0)
            if chained:
                mixed = mixed + block_of(mix_before[b]).astype(F32)
                back = back + block_of(back_before[b]).astype(F32)
                extra = extra + back_before[b][1][HALF:, :].astype(F32)
            mixed, back = mixed.astype(BF16), back.astype(BF16)
            mix_refs[b][0][...] = mixed[:HALF]
            mix_refs[b][1][:HALF, :] = mixed[HALF:]
            mix_refs[b][1][HALF:, :] = jnp.zeros((EXTRA, D), BF16)
            back_refs[b][0][...] = back[:HALF]
            back_refs[b][1][:HALF, :] = back[HALF:]
            back_refs[b][1][HALF:, :] = extra.astype(BF16)

        @pl.when(step == steps - 1)
        def _():
            weight_grad_ref[:, : 2 * FF] = gu_total[...].astype(BF16)
            for s, q in squares:
                weight_grad_ref[
                    s * size : (s + 1) * size, 2 * FF + q * size : 2 * FF + (q + 1) * size
                ] = down_total[q * size : (q + 1) * size, s * size : (s + 1) * size].astype(BF16)

    second = (lambda s: (s % 2 * 2 + s // 2, 0)) if turned else (lambda s: (s, 0))
    row_specs = [
        pl.BlockSpec((HALF, D), lambda s: (s, 0)),
        pl.BlockSpec((HALF + EXTRA, D), second),
    ] * 4
    weight_spec = pl.BlockSpec((D, 3 * FF), lambda s: (0, 0), pipeline_mode=pl.Buffered(1))
    rows_shape = [jax.ShapeDtypeStruct(part.shape, BF16) for part in rows[0]] * 4
    extra = [part for both in before for pair_ in both for part in pair_] if chained else []
    outs = pl.pallas_call(
        body,
        grid=(steps,),
        in_specs=[pl.BlockSpec(memory_space=pltpu.SMEM)]
        + row_specs * 2
        + [weight_spec]
        + row_specs * (len(extra) // 8),
        out_specs=row_specs * 2 + [weight_spec],
        out_shape=rows_shape * 2
        + [jax.ShapeDtypeStruct((D, 3 * FF), BF16)],
        scratch_shapes=[
            pltpu.VMEM((FF, D), BF16),
            pltpu.VMEM((D, 2 * FF), F32),
            pltpu.VMEM((FF, D), F32),
        ],
        compiler_params=pltpu.CompilerParams(vmem_limit_bytes=60 * 1024 * 1024),
        cost_estimate=pl.CostEstimate(flops=1000, bytes_accessed=1000, transcendentals=0),
        name="experts",
    )(expert, *sum(rows, ()), *sum(grads, ()), weights, *extra)
    parts = [(outs[k], outs[k + 1]) for k in range(0, 16, 2)]
    return parts[0:4], parts[4:8], outs[16]


def with_extra(block, low):
    count = TOPK * BLOCK // D
    lines = [part.reshape(count, D).astype(BF16) for part in low]
    lines.append(jnp.zeros((EXTRA - count * len(low), D), BF16))
    return jnp.concatenate([block] + lines, axis=0)


def halves_sum(one, other):
    count = one.shape[0] // 2
    return [
        (one[at : at + count].astype(F32) + other[at : at + count].astype(F32)).astype(BF16)
        for at in (0, count)
    ]


class Cube:
    turned = True

    def __init__(self, experts_here):
        self.place = lax.axis_index("expert")
        self.line = lax.axis_index("dp")
        self.odd = lax.rem(self.line, 2)
        self.share = experts_here // 2
        self.shards = 4
        self.own_ids = experts_here * self.place + self.share * self.odd + jnp.arange(self.share)

    def spread(self, block):
        first, second = block[:HALF], block[HALF:]
        first = jnp.concatenate([first, swap(first, "expert", X_WAY)])
        second = jnp.concatenate([second, swap(second, "expert", Y_WAY)])
        return first, swap(first, "expert", Y_WAY), second, swap(second, "expert", X_WAY)

    def cross(self, block):
        return swap(block, "dp", 1)

    def both_cores(self, near, far):
        found = []
        for first, first_y, second, second_x in (near, far):
            first = jnp.concatenate([first, first_y])
            second = jnp.concatenate([second, second_x])
            found.append((first, second))
            found.append((swap(first, "expert", CORE), swap(second, "expert", CORE)))
        return found


    def fold_cores(self, parts):
        near, near_other, far, far_other = parts

        def fold(one, other):
            return [halves_sum(a, swap(b, "expert", CORE)) for a, b in zip(one, other)]

        return fold(far, far_other), fold(near, near_other)

    def fold_once(self, parts):
        return [
            [
                halves_sum(kept, swap(sent, "expert", way))
                for (kept, sent), way in zip(part, (Y_WAY, X_WAY))
            ]
            for part in parts
        ]

    def fold_twice(self, folded):
        blocks = []
        for part in folded:
            sums = [
                kept.astype(F32) + swap(sent, "expert", way).astype(F32)
                for (kept, sent), way in zip(part, (X_WAY, Y_WAY))
            ]
            blocks.append(jnp.concatenate(sums, axis=0).astype(BF16))
        return blocks

    def fold_planes(self, blocks):
        far, near = blocks
        return near.astype(F32) + swap(far, "dp", 1).astype(F32)

    def weight(self, shards, e):
        low, high = shards[e], shards[self.share + e]
        sent = jnp.stack([low, high, low, high])
        whole = lax.all_to_all(sent, "dp", split_axis=0, concat_axis=0, tiled=True)
        return whole.reshape(D, 3 * FF)

    def weight_grad(self, total, half):
        parts = jnp.split(total.reshape(4, D // 4, 3 * FF), 2, axis=1)[half]
        return lax.all_to_all(parts, "dp", split_axis=0, concat_axis=0, tiled=True)

    def weight_grads(self, arrived):
        arrived = [jnp.concatenate(halves, axis=1) for halves in arrived]
        low = [got[0].astype(F32) + got[2].astype(F32) for got in arrived]
        high = [got[1].astype(F32) + got[3].astype(F32) for got in arrived]
        return jnp.stack(low + high)

    def gather_dense(self, shard):
        part, width = shard.shape[0] // 8, shard.shape[1]
        middle = width // 256 * 128
        own = lax.dynamic_slice_in_dim(shard, self.place * part, part, 0)[None]
        lines = jnp.concatenate([own] + [swap(own, "dp", mask) for mask in (1, 2, 3)])
        first, second = lines[..., :middle], lines[..., middle:]
        first_x, second_y = swap(first, "expert", X_WAY), swap(second, "expert", Y_WAY)
        first_y, second_x = swap(first, "expert", Y_WAY), swap(second, "expert", X_WAY)
        first_xy, second_xy = swap(first_x, "expert", Y_WAY), swap(second_y, "expert", X_WAY)
        found = (
            (lines, 0, 0),
            (first_x, 0, X_WAY),
            (second_y, middle, Y_WAY),
            (first_y, 0, Y_WAY),
            (second_x, middle, X_WAY),
            (first_xy, 0, X_WAY | Y_WAY),
            (second_xy, middle, X_WAY | Y_WAY),
        )
        parts = []
        shard_of = self.line ^ jnp.arange(4, dtype=jnp.int32)
        for piece, at, mask in found:
            for other in (0, CORE):
                held = swap(piece, "expert", CORE) if other else piece
                parts.append((held, at, (shard_of * 8 + (self.place ^ (mask | other))) * part))
        return parts, (first_x, second_y)


    def fold_dense(self, totals, first):
        core, x, y = [lax.rem(lax.div(self.place, way), 2) for way in (CORE, X_WAY, Y_WAY)]

        def fold(value, bit, axis, mask):
            kept = lax.dynamic_index_in_dim(value, bit, axis, keepdims=False)
            sent = lax.dynamic_index_in_dim(value, 1 - bit, axis, keepdims=False)
            return (kept.astype(F32) + swap(sent, "expert", mask).astype(F32)).astype(BF16)

        found = []
        for total, x_first in zip(totals, (False, True)):
            width, part = total.shape[1], total.shape[0] // 32
            lines = fold(total.reshape(4, 2, 2, 2, part, width), core, 3, CORE)
            found.append(fold(lines, x, 2, X_WAY) if x_first else fold(lines, y, 1, Y_WAY))
        found, first = lax.optimization_barrier((found, first))
        return [fold(found[0], x, 1, X_WAY), fold(found[1], y, 1, Y_WAY)], first

    def sum_dense(self, found):
        lines = jnp.concatenate(found, axis=-1)
        summed = lax.dynamic_index_in_dim(lines, self.line, 0).astype(F32)
        for mask in (1, 2, 3):
            sent = lax.dynamic_index_in_dim(lines, self.line ^ mask, 0)
            summed = summed + swap(sent, "dp", mask).astype(F32)
        return summed.astype(BF16)

    def spread_dense(self, summed):
        _, part, width = summed.shape
        whole = jnp.zeros((8, part, width), BF16)
        for mask in range(8):
            piece = swap(summed, "expert", mask) if mask else summed
            whole = lax.dynamic_update_slice(whole, piece, (self.place ^ mask, 0, 0))
        return whole.reshape(-1, width).astype(F32)


class Plain:
    turned = False

    def __init__(self, experts_here):
        self.share = experts_here
        self.shards = lax.axis_size("dp")
        self.own_ids = experts_here * lax.axis_index("expert") + jnp.arange(experts_here)

    def spread(self, block):
        return block

    def cross(self, block):
        return block

    def both_cores(self, near, far):
        halves = [
            jnp.split(lax.all_gather(half, "expert", axis=0, tiled=True), 4, axis=0)
            for half in (near[:HALF], near[HALF:])
        ]
        return list(zip(*halves))

    def fold_cores(self, parts):
        return [
            tuple(
                lax.psum_scatter(
                    jnp.concatenate(halves), "expert", scatter_dimension=0, tiled=True
                )
                for halves in zip(*parts)
            )
        ]

    def fold_once(self, parts):
        return parts

    def fold_twice(self, parts):
        return [jnp.concatenate(part, axis=0) for part in parts]

    def fold_planes(self, blocks):
        return blocks[0].astype(F32)

    def gather_dense(self, shard):
        part = shard.shape[0] // lax.axis_size("expert")
        own = lax.dynamic_slice_in_dim(shard, lax.axis_index("expert") * part, part, 0)
        whole = lax.all_gather(own, ("dp", "expert"), axis=0, tiled=True)
        return [(whole[None], 0, jnp.zeros((1,), jnp.int32))], own

    def weight(self, shards, e):
        return lax.all_gather(shards[e], "dp", axis=0, tiled=True)

    def weight_grad(self, total, half):
        parts = jnp.split(total.reshape(self.shards, -1, 3 * FF), 2, axis=1)[half]
        return lax.psum_scatter(parts, "dp", scatter_dimension=0)

    def weight_grads(self, arrived):
        return jnp.stack([jnp.concatenate(halves, axis=0) for halves in arrived]).astype(F32)

    def fold_dense(self, totals, first):
        both = ("dp", "expert")
        return [lax.psum_scatter(t, both, scatter_dimension=0, tiled=True) for t in totals], first

    def sum_dense(self, sums):
        return jnp.concatenate(sums, axis=-1)

    def spread_dense(self, sums):
        return lax.all_gather(sums, "expert", axis=0, tiled=True).astype(F32)


def on_device(
    tokens,
    routes,
    lengths,
    query_weight,
    key_weight,
    value_weight,
    output_weight,
    router_weight,
    first_gain,
    second_gain,
    expert_gate,
    expert_up,
    expert_down,
    cotangent,
):
    tok_count = tokens.shape[0]
    here = expert_gate.shape[0]
    cube = lax.axis_size("dp") == 4 and lax.axis_size("expert") == 8 and here % 2 == 0
    plan = Cube(here) if cube else Plain(here)

    small = jnp.concatenate(
        [
            router_weight,
            first_gain[:, None],
            second_gain[:, None],
            jnp.zeros((router_weight.shape[0], 128 - EXPERTS - 2), BF16),
        ],
        axis=1,
    )
    grad_block = with_extra(cotangent, [routes.T.astype(F32)])
    grad_near = plan.spread(grad_block)
    dense_parts, lines = plan.gather_dense(
        jnp.concatenate([query_weight, key_weight, value_weight, output_weight, small], axis=1)
    )
    grad_across = plan.cross(grad_block)
    grad_far = plan.spread(tie(grad_across, dense_parts[-1][0]))
    shards = pack_weights(expert_gate, expert_up, expert_down)
    weights = [plan.weight(tie(shards, lines, grad_across), 0)]

    cosine, sine = layout_tables(lengths[0], tok_count)
    cosine, sine = jnp.concatenate([cosine, cosine], axis=1), jnp.concatenate([sine, sine], axis=1)
    kept = forward_call(lengths[0], tokens, dense_parts, cosine, sine)
    residual, normed_two, logits, dense = kept[6:]
    logits = logits[:, :EXPERTS]
    choose = (routes[:, :, None] == jnp.arange(EXPERTS, dtype=jnp.int32)[None, None, :]).astype(F32)
    chosen = jnp.sum(choose * logits[:, None, :], axis=-1)
    top_chosen = jnp.max(chosen, axis=-1, keepdims=True)
    raised_gates = jnp.exp(chosen - top_chosen)
    gates = raised_gates / jnp.sum(raised_gates, axis=-1, keepdims=True)

    gate_lines = gates.T
    gate_high = lax.optimization_barrier(gate_lines.astype(BF16))
    gate_low = gate_lines - gate_high.astype(F32)
    block, grad_near, grad_far, weights = lax.optimization_barrier(
        (with_extra(normed_two, [gate_high, gate_low]), grad_near, grad_far, weights)
    )
    rows_near, rows_across = lax.optimization_barrier((plan.spread(block), plan.cross(block)))
    rows = plan.both_cores(rows_near, plan.spread(rows_across))
    grad_rows = plan.both_cores(grad_near, grad_far)
    for e in range(1, plan.share):
        weights.append(plan.weight(tie(shards, rows_across, weights[-1]), e))

    done, weight_parts = None, []
    for e in range(plan.share):
        mixes, backs, weight_part = expert_call(
            plan.own_ids[e : e + 1].astype(jnp.int32),
            rows,
            grad_rows,
            weights[e],
            plan.shards,
            plan.turned,
            done,
        )
        done = (mixes, backs)
        if e < plan.share - 1:
            weight_parts.append([plan.weight_grad(weight_part, 0)])
        if e > 0:
            done, weight_parts[e - 1] = lax.optimization_barrier((done, weight_parts[e - 1]))
        if e < plan.share - 1:
            last = weight_part
    arrived = weight_parts
    if plan.share > 1:
        arrived[-1].append(plan.weight_grad(tie(last, arrived[-1]), 1))
    folded = plan.fold_once(plan.fold_cores(done[1]))
    mixes = plan.fold_cores(done[0])
    folded, mixes, arrived = lax.optimization_barrier((folded, mixes, arrived))
    folded = plan.fold_twice(folded)
    mixes = plan.fold_once(tie(mixes, folded))
    back_held = plan.fold_planes(folded)
    back_rows = back_held[:BLOCK]
    owners_back = back_held[BLOCK : BLOCK + EXTRA // 2] + back_held[BLOCK + EXTRA // 2 :]
    owners_back = owners_back.reshape(EXPERTS, BLOCK)
    arrived.append([plan.weight_grad(tie(weight_part, back_rows), 0)])

    gate_back = jnp.sum(choose * owners_back.T[:, None, :], axis=-1)
    chosen_back = gates * (gate_back - jnp.sum(gates * gate_back, axis=-1, keepdims=True))
    logit_back = jnp.sum(chosen_back[:, :, None] * choose, axis=1).astype(BF16)
    logit_back = jnp.pad(logit_back, ((0, 0), (0, 128 - EXPERTS)))
    input_grad, late, early = backward_call(
        lengths[0], tokens, cotangent, dense, cosine, sine, kept, logit_back, back_rows
    )
    late, early, mixes, arrived = lax.optimization_barrier((late, early, mixes, arrived))
    arrived[-1].append(plan.weight_grad(tie(weight_part, arrived[-1]), 1))
    sums, (arrived, mixes) = plan.fold_dense([late, early], (arrived, plan.fold_twice(mixes)))
    mixture = plan.fold_planes(tie(mixes, sums))
    output = (residual + mixture[:BLOCK]).astype(BF16)
    dense_grad = plan.spread_dense(plan.sum_dense(sums))
    weight_grad = plan.weight_grads(arrived)
    return (
        output,
        input_grad,
        dense_grad[:, :HD],
        dense_grad[:, HD : HD + KVD],
        dense_grad[:, HD + KVD : QKV],
        dense_grad[:, QKV + 128 :],
        dense_grad[:, QKV : QKV + EXPERTS],
        dense_grad[:, QKV + EXPERTS],
        dense_grad[:, QKV + EXPERTS + 1],
        weight_grad[:, :, :FF],
        weight_grad[:, :, FF : 2 * FF],
        jnp.concatenate(
            jnp.split(weight_grad[:, :, 2 * FF :], FF // weight_grad.shape[1], axis=2), axis=1
        ),
    )


def solution(mesh):
    return jax.shard_map(
        on_device,
        mesh=mesh,
        in_specs=(
            P(("dp", "expert"), None),
            P(("dp", "expert"), None),
            P(("dp", "expert"), None),
            P("dp", None),
            P("dp", None),
            P("dp", None),
            P("dp", None),
            P("dp", None),
            P("dp"),
            P("dp"),
            P("expert", "dp", None),
            P("expert", "dp", None),
            P("expert", None, "dp"),
            P(("dp", "expert"), None),
        ),
        out_specs=(
            P(("dp", "expert"), None),
            P(("dp", "expert"), None),
            P("dp", None),
            P("dp", None),
            P("dp", None),
            P("dp", None),
            P("dp", None),
            P("dp"),
            P("dp"),
            P("expert", "dp", None),
            P("expert", "dp", None),
            P("expert", None, "dp"),
        ),
        check_vma=False,
    )
```

```python
import jax
import jax.numpy as jnp
from jax import lax
from jax.experimental import pallas as pl
from jax.experimental.pallas import tpu as pltpu
from jax.sharding import PartitionSpec as P

D = 1024
HEADS = 16
KV_HEADS = 8
HEAD_DIM = 64
EXPERTS = 32
TOPK = 8
CAP = 128
FF = 512
BLOCK = 256
EXTRA = 16
HELD = BLOCK + EXTRA
HALF = BLOCK // 2
HD = HEADS * HEAD_DIM
KVD = KV_HEADS * HEAD_DIM

EPSILON = 1e-06
THETA = 10000.0
F32 = jnp.float32
BF16 = jnp.bfloat16

CORE, X_WAY, Y_WAY = 1, 2, 4


def layout_tables(length_row, count):
    places = jnp.arange(count, dtype=jnp.int32)
    ends = jnp.cumsum(length_row)
    passed = places[:, None] >= ends[None, :]
    begins = jnp.sum(jnp.where(passed, length_row[None, :], 0), axis=1)
    position = (places - begins).astype(F32)
    frequency = THETA ** (-(jnp.arange(HEAD_DIM // 2, dtype=F32) * 2.0 / HEAD_DIM))
    angles = position[:, None] * frequency[None, :]
    cosine = jnp.concatenate([jnp.cos(angles), jnp.cos(angles)], axis=-1)
    sine = jnp.concatenate([jnp.sin(angles), jnp.sin(angles)], axis=-1)
    return (cosine, sine)


def contract_rows(left, right):
    return lax.dot_general(left, right, (((0,), (0,)), ((), ())), preferred_element_type=F32)


def times_transpose(left, right):
    return lax.dot_general(left, right, (((1,), (1,)), ((), ())), preferred_element_type=F32)


def times(left, right):
    return jnp.dot(left, right, preferred_element_type=F32)


def rotate(values):
    width = values.shape[1]
    lane = lax.broadcasted_iota(jnp.int32, values.shape, 1)
    half = HEAD_DIM // 2
    return jnp.where(
        lax.rem(lane, HEAD_DIM) < half,
        -pltpu.roll(values, width - half, 1),
        pltpu.roll(values, half, 1),
    )


def wide(table, width):
    return jnp.concatenate([table] * (width // table.shape[1]), axis=1)


def allowed_pairs(length_ref, count):
    row = lax.broadcasted_iota(jnp.int32, (count, count), 0)
    column = lax.broadcasted_iota(jnp.int32, (count, count), 1)
    allowed = column <= row
    end = 0
    for s in range(length_ref.shape[0] - 1):
        end = end + length_ref[s]
        allowed = allowed & ((row >= end) == (column >= end))
    allowed = jnp.where(allowed, 1.0, 0.0)
    return jnp.concatenate([allowed, allowed], axis=0) > 0.0


def pair(value, h):
    at = 2 * HEAD_DIM * h
    return jnp.concatenate(
        [value[:, at : at + HEAD_DIM], value[:, at + HEAD_DIM : at + 2 * HEAD_DIM]], axis=0
    )


def beside(value):
    count = value.shape[0] // 2
    return jnp.concatenate([value[:count], value[count:]], axis=1)


def key_head(value, h):
    return value[:, HEAD_DIM * h : HEAD_DIM * (h + 1)]


def gains(dense_ref):
    lines = dense_ref[:, 3 * D :].astype(F32).T
    return lines[EXPERTS : EXPERTS + 1], lines[EXPERTS + 1 : EXPERTS + 2]


SCALE = HEAD_DIM ** (-0.5)
QKV = HD + 2 * KVD
WHOLE = pl.BlockSpec(memory_space=pltpu.VMEM)
SCALARS = pl.BlockSpec(memory_space=pltpu.SMEM)


def forward_call(lengths, tokens, parts, cosine, sine):
    count = tokens.shape[0]
    columns = [at for _, at, _ in parts]
    starts = jnp.concatenate([start for _, _, start in parts]).astype(jnp.int32)
    parts = [part for part, _, _ in parts]

    def body(length_ref, start_ref, token_ref, cos_ref, sin_ref, *refs):
        part_refs, outs = refs[: len(parts)], refs[len(parts) :]
        n1_ref, q_ref, k_ref, v_ref, att_ref, lse_ref, res_ref, n2_ref, logit_ref, dense_ref = outs
        for p, part_ref in enumerate(part_refs):
            pieces, rows, width = part_ref.shape
            for s in range(pieces):
                start = pl.multiple_of(start_ref[p * pieces + s], rows)
                dense_ref[pl.ds(start, rows), columns[p] : columns[p] + width] = part_ref[s]
        gain_a, gain_b = gains(dense_ref)
        x = token_ref[...].astype(F32)
        r1 = lax.rsqrt(jnp.mean(x * x, axis=1, keepdims=True) + EPSILON)
        n1 = (x * r1 * gain_a).astype(BF16)
        n1_ref[...] = n1
        qkv = times(n1, dense_ref[:, :QKV])
        q_lin, k_lin = qkv[:, :HD], qkv[:, HD : HD + KVD]
        cos, sin = wide(cos_ref[...], HD), wide(sin_ref[...], HD)
        q = ((q_lin * cos + rotate(q_lin) * sin) * SCALE).astype(BF16)
        k = (k_lin * cos[:, :KVD] + rotate(k_lin) * sin[:, :KVD]).astype(BF16)
        v = qkv[:, HD + KVD :].astype(BF16)
        q_ref[...], k_ref[...], v_ref[...] = q, k, v
        allowed = allowed_pairs(length_ref, count)
        lane = lax.broadcasted_iota(jnp.int32, (count, 128), 1)
        lse = jnp.zeros((count, 128), F32)
        for h in range(KV_HEADS):
            scores = times_transpose(pair(q, h), key_head(k, h))
            scores = jnp.where(allowed, scores, -1e30)
            highest = jnp.max(scores, axis=1, keepdims=True)
            raised = jnp.exp(scores - highest)
            total = jnp.sum(raised, axis=1, keepdims=True)
            probs = (raised / total).astype(BF16)
            mixed = times(probs, key_head(v, h))
            att_ref[:, 2 * HEAD_DIM * h : 2 * HEAD_DIM * (h + 1)] = beside(mixed).astype(BF16)
            logs = highest + jnp.log(total)
            lse = jnp.where(lane == 2 * h, logs[:count], lse)
            lse = jnp.where(lane == 2 * h + 1, logs[count:], lse)
        lse_ref[...] = lse
        residual = x + times(att_ref[...], dense_ref[:, QKV : QKV + D])
        res_ref[...] = residual
        r2 = lax.rsqrt(jnp.mean(residual * residual, axis=1, keepdims=True) + EPSILON)
        n2 = (residual * r2 * gain_b).astype(BF16)
        n2_ref[...] = n2
        logit_ref[...] = times(n2, dense_ref[:, 3 * D :])

    def out(width, dtype):
        return jax.ShapeDtypeStruct((count, width), dtype)

    return pl.pallas_call(
        body,
        in_specs=[SCALARS] * 2 + [WHOLE] * (3 + len(parts)),
        out_specs=[WHOLE] * 10,
        out_shape=[
            out(D, BF16), out(HD, BF16), out(KVD, BF16), out(KVD, BF16), out(HD, BF16),
            out(128, F32), out(D, F32), out(D, BF16), out(128, F32),
            jax.ShapeDtypeStruct((D, 3 * D + 128), BF16),
        ],
        compiler_params=pltpu.CompilerParams(vmem_limit_bytes=56 * 1024 * 1024),
        cost_estimate=pl.CostEstimate(flops=1000, bytes_accessed=1000, transcendentals=0),
        name="attention_forward",
    )(lengths, starts, tokens, cosine, sine, *parts)


def backward_call(lengths, tokens, cotangent, dense, cosine, sine, kept, logit_back, back_rows):
    count = tokens.shape[0]

    def body(
        length_ref, token_ref, dy_ref, dense_ref, cos_ref, sin_ref,
        n1_ref, q_ref, k_ref, v_ref, att_ref, lse_ref, res_ref, n2_ref, lb_ref, back_ref,
        input_ref, late_ref, early_ref,
    ):
        gain_a, gain_b = gains(dense_ref)
        residual = res_ref[...]
        r2 = lax.rsqrt(jnp.mean(residual * residual, axis=1, keepdims=True) + EPSILON)
        back = times_transpose(lb_ref[...], dense_ref[:, 3 * D :]) + back_ref[...]
        second_terms = (back * residual * r2).astype(BF16)
        scaled = back * gain_b
        residual_back = (
            dy_ref[...].astype(F32)
            + r2 * scaled
            - residual * (r2 * r2 * r2) * jnp.mean(scaled * residual, axis=1, keepdims=True)
        )
        branch_back = residual_back.astype(BF16)
        early_ref[...] = contract_rows(att_ref[...], branch_back).astype(BF16)
        att_back = times_transpose(branch_back, dense_ref[:, QKV : QKV + D]).astype(BF16)
        q, k, v, lse = q_ref[...], k_ref[...], v_ref[...], lse_ref[...]
        allowed = allowed_pairs(length_ref, count)
        q_back, k_back, v_back = [], [], []
        for h in range(KV_HEADS):
            queries, keys, values = pair(q, h), key_head(k, h), key_head(v, h)
            grads = pair(att_back, h)
            logs = jnp.concatenate([lse[:, 2 * h : 2 * h + 1], lse[:, 2 * h + 1 : 2 * h + 2]], axis=0)
            scores = jnp.where(allowed, times_transpose(queries, keys), -1e30)
            probs = jnp.exp(scores - logs)
            prob_back = times_transpose(grads, values)
            spread = jnp.sum(prob_back * probs, axis=1, keepdims=True)
            score_back = (probs * (prob_back - spread)).astype(BF16)
            q_back.append(beside(times(score_back, keys)))
            k_back.append(contract_rows(score_back, queries))
            v_back.append(contract_rows(probs.astype(BF16), grads))
        q_back = jnp.concatenate(q_back, axis=1)
        k_back = jnp.concatenate(k_back, axis=1)
        v_back = jnp.concatenate(v_back, axis=1)
        cos, sin = wide(cos_ref[...], HD), wide(sin_ref[...], HD)
        q_back = ((q_back * cos - rotate(q_back * sin)) * SCALE).astype(BF16)
        k_back = (k_back * cos[:, :KVD] - rotate(k_back * sin[:, :KVD])).astype(BF16)
        qkv_back = jnp.concatenate([q_back, k_back, v_back.astype(BF16)], axis=1)
        late_ref[:, :QKV] = contract_rows(n1_ref[...], qkv_back).astype(BF16)
        first_back = times_transpose(qkv_back, dense_ref[:, :QKV])
        x = token_ref[...].astype(F32)
        r1 = lax.rsqrt(jnp.mean(x * x, axis=1, keepdims=True) + EPSILON)
        first_terms = (first_back * x * r1).astype(BF16)
        scaled = first_back * gain_a
        input_ref[...] = (
            residual_back
            + r1 * scaled
            - x * (r1 * r1 * r1) * jnp.mean(scaled * x, axis=1, keepdims=True)
        )
        lane = lax.broadcasted_iota(jnp.int32, (count, 128), 1)
        marks = [jnp.where(lane == EXPERTS + s, 1.0, 0.0).astype(BF16) for s in (0, 1)]
        late_ref[:, QKV:] = (
            contract_rows(n2_ref[...], lb_ref[...])
            + contract_rows(first_terms, marks[0])
            + contract_rows(second_terms, marks[1])
        ).astype(BF16)

    return pl.pallas_call(
        body,
        in_specs=[SCALARS] + [WHOLE] * 15,
        out_specs=[WHOLE] * 3,
        out_shape=[
            jax.ShapeDtypeStruct((count, D), F32),
            jax.ShapeDtypeStruct((D, QKV + 128), BF16),
            jax.ShapeDtypeStruct((D, D), BF16),
        ],
        compiler_params=pltpu.CompilerParams(vmem_limit_bytes=56 * 1024 * 1024),
        cost_estimate=pl.CostEstimate(flops=50 * 10**9, bytes_accessed=10**7, transcendentals=0),
        name="attention_backward",
    )(lengths, tokens, cotangent, dense, cosine, sine, *kept[:8], logit_back, back_rows)


def swap(value, axis, mask):
    size = lax.axis_size(axis)
    return lax.ppermute(value, axis, [(k, k ^ mask) for k in range(size)])


def tie(value, *first):
    return lax.optimization_barrier((value, first))[0]


def pack_weights(gate, up, down):
    rows = gate.shape[1]
    parts = [down[:, at : at + rows] for at in range(0, FF, rows)]
    return jnp.concatenate([gate, up] + parts, axis=2)


def expert_call(expert, rows, grads, weights, shards, turned, before):
    steps = rows[0][0].shape[0] // HALF
    chained = before is not None
    size = D // shards
    squares = [(s, q) for s in range(shards) for q in range(FF // size)]

    def body(expert_ref, *refs):
        def pairs(at):
            return [refs[at + 2 * b : at + 2 * b + 2] for b in range(4)]

        row_refs, grad_refs, weight_ref = pairs(0), pairs(8), refs[16]
        at = 17
        if chained:
            mix_before, back_before = pairs(17), pairs(25)
            at = 33
        mix_refs, back_refs = pairs(at), pairs(at + 8)
        weight_grad_ref, down, gu_total, down_total = refs[at + 16 :]

        def block_of(pair_refs):
            return jnp.concatenate([pair_refs[0][...], pair_refs[1][:HALF, :]], axis=0)
        step = pl.program_id(0)

        @pl.when(step == 0)
        def _():
            gu_total[...] = jnp.zeros_like(gu_total)
            down_total[...] = jnp.zeros_like(down_total)
            for s, q in squares:
                down[q * size : (q + 1) * size, s * size : (s + 1) * size] = weight_ref[
                    s * size : (s + 1) * size, 2 * FF + q * size : 2 * FF + (q + 1) * size
                ]

        def by_token(value):
            value = value[0:1] + value[1:2]
            return sum(value[:, at : at + BLOCK] for at in range(0, D, BLOCK))

        counts, gate_lines = [], []
        for b in range(4):
            named = grad_refs[b][1][HALF:, :].astype(F32)[0:2] == expert_ref[0].astype(F32)
            gates = row_refs[b][1][HALF:, :].astype(F32)
            gates = gates[0:2] + gates[2:4]
            counts.append(by_token(jnp.where(named, 1.0, 0.0)))
            gate_lines.append(by_token(jnp.where(named, gates, 0.0)))
        hit = jnp.concatenate(counts + [jnp.zeros((4, BLOCK), F32)], axis=0)
        earlier = lax.broadcasted_iota(jnp.int32, (BLOCK, BLOCK), 0) < lax.broadcasted_iota(
            jnp.int32, (BLOCK, BLOCK), 1
        )
        slots = times(hit.astype(BF16), jnp.where(earlier, 1.0, 0.0).astype(BF16))
        slots = jnp.where(hit > 0.0, slots, -1.0).astype(jnp.int32)
        slot_ids = lax.broadcasted_iota(jnp.int32, (CAP, BLOCK), 0)
        hots, hots_low, z, raw, gate_cols = [], [], [], [], []
        for b in range(4):
            hot = slots[b : b + 1] == slot_ids
            hot_low = jnp.where(hot, 1.0, 0.0).astype(BF16)
            z.append(times(hot_low, block_of(row_refs[b])).astype(BF16))
            raw.append(times(hot_low, block_of(grad_refs[b])))
            gate_cols.append(
                jnp.sum(jnp.where(hot, gate_lines[b], 0.0), axis=1, keepdims=True)
            )
            hots.append(hot)
            hots_low.append(hot_low)
        z = jnp.concatenate(z, axis=0)
        raw = jnp.concatenate(raw, axis=0)
        gate_col = jnp.concatenate(gate_cols, axis=0)
        both = times(z, weight_ref[:, : 2 * FF])
        gate_pre, up_pre = both[:, :FF], both[:, FF:]
        sigma = jax.nn.sigmoid(gate_pre)
        activated = gate_pre * sigma
        hidden = (activated * up_pre).astype(BF16)
        produced = times(hidden, down[...]).astype(BF16).astype(F32)
        gate_back = jnp.sum(raw * produced, axis=1, keepdims=True)
        weighted = (gate_col * produced).astype(BF16)
        slot_back = (gate_col * raw).astype(BF16)
        hidden_back = times_transpose(slot_back, down[...])
        gate_slope = (hidden_back * up_pre * sigma * (1.0 + gate_pre * (1.0 - sigma))).astype(BF16)
        up_slope = (hidden_back * activated).astype(BF16)
        slopes = jnp.concatenate([gate_slope, up_slope], axis=1)
        gu_total[...] += contract_rows(z, slopes)
        down_total[...] += contract_rows(hidden, slot_back)
        entry_back = times_transpose(slopes, weight_ref[:, : 2 * FF]).astype(BF16)
        ranks = lax.broadcasted_iota(jnp.int32, (EXPERTS // 4, BLOCK), 0)
        for b in range(4):
            part = slice(b * CAP, (b + 1) * CAP)
            mixed = contract_rows(hots_low[b], weighted[part])
            back = contract_rows(hots_low[b], entry_back[part])
            line = jnp.sum(jnp.where(hots[b], gate_back[part], 0.0), axis=0, keepdims=True)
            extra = jnp.concatenate(
                [jnp.where(ranks * 4 + q == expert_ref[0], line, 0.0) for q in range(4)], axis=1
            )
            high = extra.astype(BF16).astype(F32)
            extra = jnp.concatenate([high, extra - high], axis=0)
            if chained:
                mixed = mixed + block_of(mix_before[b]).astype(F32)
                back = back + block_of(back_before[b]).astype(F32)
                extra = extra + back_before[b][1][HALF:, :].astype(F32)
            mixed, back = mixed.astype(BF16), back.astype(BF16)
            mix_refs[b][0][...] = mixed[:HALF]
            mix_refs[b][1][:HALF, :] = mixed[HALF:]
            mix_refs[b][1][HALF:, :] = jnp.zeros((EXTRA, D), BF16)
            back_refs[b][0][...] = back[:HALF]
            back_refs[b][1][:HALF, :] = back[HALF:]
            back_refs[b][1][HALF:, :] = extra.astype(BF16)

        @pl.when(step == steps - 1)
        def _():
            weight_grad_ref[:, : 2 * FF] = gu_total[...].astype(BF16)
            for s, q in squares:
                weight_grad_ref[
                    s * size : (s + 1) * size, 2 * FF + q * size : 2 * FF + (q + 1) * size
                ] = down_total[q * size : (q + 1) * size, s * size : (s + 1) * size].astype(BF16)

    second = (lambda s: (s % 2 * 2 + s // 2, 0)) if turned else (lambda s: (s, 0))
    row_specs = [
        pl.BlockSpec((HALF, D), lambda s: (s, 0)),
        pl.BlockSpec((HALF + EXTRA, D), second),
    ] * 4
    weight_spec = pl.BlockSpec((D, 3 * FF), lambda s: (0, 0), pipeline_mode=pl.Buffered(1))
    rows_shape = [jax.ShapeDtypeStruct(part.shape, BF16) for part in rows[0]] * 4
    extra = [part for both in before for pair_ in both for part in pair_] if chained else []
    outs = pl.pallas_call(
        body,
        grid=(steps,),
        in_specs=[pl.BlockSpec(memory_space=pltpu.SMEM)]
        + row_specs * 2
        + [weight_spec]
        + row_specs * (len(extra) // 8),
        out_specs=row_specs * 2 + [weight_spec],
        out_shape=rows_shape * 2
        + [jax.ShapeDtypeStruct((D, 3 * FF), BF16)],
        scratch_shapes=[
            pltpu.VMEM((FF, D), BF16),
            pltpu.VMEM((D, 2 * FF), F32),
            pltpu.VMEM((FF, D), F32),
        ],
        compiler_params=pltpu.CompilerParams(vmem_limit_bytes=60 * 1024 * 1024),
        cost_estimate=pl.CostEstimate(flops=1000, bytes_accessed=1000, transcendentals=0),
        name="experts",
    )(expert, *sum(rows, ()), *sum(grads, ()), weights, *extra)
    parts = [(outs[k], outs[k + 1]) for k in range(0, 16, 2)]
    return parts[0:4], parts[4:8], outs[16]


def with_extra(block, low):
    count = TOPK * BLOCK // D
    lines = [part.reshape(count, D).astype(BF16) for part in low]
    lines.append(jnp.zeros((EXTRA - count * len(low), D), BF16))
    return jnp.concatenate([block] + lines, axis=0)


def halves_sum(one, other):
    count = one.shape[0] // 2
    return [
        (one[at : at + count].astype(F32) + other[at : at + count].astype(F32)).astype(BF16)
        for at in (0, count)
    ]


class Cube:
    turned = True

    def __init__(self, experts_here):
        self.place = lax.axis_index("expert")
        self.line = lax.axis_index("dp")
        self.odd = lax.rem(self.line, 2)
        self.share = experts_here // 2
        self.shards = 4
        self.own_ids = experts_here * self.place + self.share * self.odd + jnp.arange(self.share)

    def spread(self, block):
        first, second = block[:HALF], block[HALF:]
        first = jnp.concatenate([first, swap(first, "expert", X_WAY)])
        second = jnp.concatenate([second, swap(second, "expert", Y_WAY)])
        return first, swap(first, "expert", Y_WAY), second, swap(second, "expert", X_WAY)

    def cross(self, block):
        return swap(block, "dp", 1)

    def both_cores(self, near, far):
        found = []
        for first, first_y, second, second_x in (near, far):
            first = jnp.concatenate([first, first_y])
            second = jnp.concatenate([second, second_x])
            found.append((first, second))
            found.append((swap(first, "expert", CORE), swap(second, "expert", CORE)))
        return found


    def fold_cores(self, parts):
        near, near_other, far, far_other = parts

        def fold(one, other):
            return [halves_sum(a, swap(b, "expert", CORE)) for a, b in zip(one, other)]

        return fold(far, far_other), fold(near, near_other)

    def fold_once(self, parts):
        return [
            [
                halves_sum(kept, swap(sent, "expert", way))
                for (kept, sent), way in zip(part, (Y_WAY, X_WAY))
            ]
            for part in parts
        ]

    def fold_twice(self, folded):
        blocks = []
        for part in folded:
            sums = [
                kept.astype(F32) + swap(sent, "expert", way).astype(F32)
                for (kept, sent), way in zip(part, (X_WAY, Y_WAY))
            ]
            blocks.append(jnp.concatenate(sums, axis=0).astype(BF16))
        return blocks

    def fold_planes(self, blocks):
        far, near = blocks
        return near.astype(F32) + swap(far, "dp", 1).astype(F32)

    def weight(self, shards, e):
        low, high = shards[e], shards[self.share + e]
        sent = jnp.stack([low, high, low, high])
        whole = lax.all_to_all(sent, "dp", split_axis=0, concat_axis=0, tiled=True)
        return whole.reshape(D, 3 * FF)

    def weight_grad(self, total, half):
        parts = jnp.split(total.reshape(4, D // 4, 3 * FF), 2, axis=1)[half]
        return lax.all_to_all(parts, "dp", split_axis=0, concat_axis=0, tiled=True)

    def weight_grads(self, arrived):
        arrived = [jnp.concatenate(halves, axis=1) for halves in arrived]
        low = [got[0].astype(F32) + got[2].astype(F32) for got in arrived]
        high = [got[1].astype(F32) + got[3].astype(F32) for got in arrived]
        return jnp.stack(low + high)

    def gather_dense(self, shard):
        part, width = shard.shape[0] // 8, shard.shape[1]
        middle = width // 256 * 128
        own = lax.dynamic_slice_in_dim(shard, self.place * part, part, 0)[None]
        lines = jnp.concatenate([own] + [swap(own, "dp", mask) for mask in (1, 2, 3)])
        first, second = lines[..., :middle], lines[..., middle:]
        first_x, second_y = swap(first, "expert", X_WAY), swap(second, "expert", Y_WAY)
        first_y, second_x = swap(first, "expert", Y_WAY), swap(second, "expert", X_WAY)
        first_xy, second_xy = swap(first_x, "expert", Y_WAY), swap(second_y, "expert", X_WAY)
        found = (
            (lines, 0, 0),
            (first_x, 0, X_WAY),
            (second_y, middle, Y_WAY),
            (first_y, 0, Y_WAY),
            (second_x, middle, X_WAY),
            (first_xy, 0, X_WAY | Y_WAY),
            (second_xy, middle, X_WAY | Y_WAY),
        )
        parts = []
        shard_of = self.line ^ jnp.arange(4, dtype=jnp.int32)
        for piece, at, mask in found:
            for other in (0, CORE):
                held = swap(piece, "expert", CORE) if other else piece
                parts.append((held, at, (shard_of * 8 + (self.place ^ (mask | other))) * part))
        return parts, (first_x, second_y)


    def fold_dense(self, totals, first):
        core, x, y = [lax.rem(lax.div(self.place, way), 2) for way in (CORE, X_WAY, Y_WAY)]

        def fold(value, bit, axis, mask):
            kept = lax.dynamic_index_in_dim(value, bit, axis, keepdims=False)
            sent = lax.dynamic_index_in_dim(value, 1 - bit, axis, keepdims=False)
            return (kept.astype(F32) + swap(sent, "expert", mask).astype(F32)).astype(BF16)

        found = []
        for total, x_first in zip(totals, (False, True)):
            width, part = total.shape[1], total.shape[0] // 32
            lines = fold(total.reshape(4, 2, 2, 2, part, width), core, 3, CORE)
            found.append(fold(lines, x, 2, X_WAY) if x_first else fold(lines, y, 1, Y_WAY))
        found, first = lax.optimization_barrier((found, first))
        return [fold(found[0], x, 1, X_WAY), fold(found[1], y, 1, Y_WAY)], first

    def sum_dense(self, found):
        lines = jnp.concatenate(found, axis=-1)
        summed = lax.dynamic_index_in_dim(lines, self.line, 0).astype(F32)
        for mask in (1, 2, 3):
            sent = lax.dynamic_index_in_dim(lines, self.line ^ mask, 0)
            summed = summed + swap(sent, "dp", mask).astype(F32)
        return summed.astype(BF16)

    def spread_dense(self, summed):
        _, part, width = summed.shape
        whole = jnp.zeros((8, part, width), BF16)
        for mask in range(8):
            piece = swap(summed, "expert", mask) if mask else summed
            whole = lax.dynamic_update_slice(whole, piece, (self.place ^ mask, 0, 0))
        return whole.reshape(-1, width).astype(F32)


class Plain:
    turned = False

    def __init__(self, experts_here):
        self.share = experts_here
        self.shards = lax.axis_size("dp")
        self.own_ids = experts_here * lax.axis_index("expert") + jnp.arange(experts_here)

    def spread(self, block):
        return block

    def cross(self, block):
        return block

    def both_cores(self, near, far):
        halves = [
            jnp.split(lax.all_gather(half, "expert", axis=0, tiled=True), 4, axis=0)
            for half in (near[:HALF], near[HALF:])
        ]
        return list(zip(*halves))

    def fold_cores(self, parts):
        return [
            tuple(
                lax.psum_scatter(
                    jnp.concatenate(halves), "expert", scatter_dimension=0, tiled=True
                )
                for halves in zip(*parts)
            )
        ]

    def fold_once(self, parts):
        return parts

    def fold_twice(self, parts):
        return [jnp.concatenate(part, axis=0) for part in parts]

    def fold_planes(self, blocks):
        return blocks[0].astype(F32)

    def gather_dense(self, shard):
        part = shard.shape[0] // lax.axis_size("expert")
        own = lax.dynamic_slice_in_dim(shard, lax.axis_index("expert") * part, part, 0)
        whole = lax.all_gather(own, ("dp", "expert"), axis=0, tiled=True)
        return [(whole[None], 0, jnp.zeros((1,), jnp.int32))], own

    def weight(self, shards, e):
        return lax.all_gather(shards[e], "dp", axis=0, tiled=True)

    def weight_grad(self, total, half):
        parts = jnp.split(total.reshape(self.shards, -1, 3 * FF), 2, axis=1)[half]
        return lax.psum_scatter(parts, "dp", scatter_dimension=0)

    def weight_grads(self, arrived):
        return jnp.stack([jnp.concatenate(halves, axis=0) for halves in arrived]).astype(F32)

    def fold_dense(self, totals, first):
        both = ("dp", "expert")
        return [lax.psum_scatter(t, both, scatter_dimension=0, tiled=True) for t in totals], first

    def sum_dense(self, sums):
        return jnp.concatenate(sums, axis=-1)

    def spread_dense(self, sums):
        return lax.all_gather(sums, "expert", axis=0, tiled=True).astype(F32)


def on_device(
    tokens,
    routes,
    lengths,
    query_weight,
    key_weight,
    value_weight,
    output_weight,
    router_weight,
    first_gain,
    second_gain,
    expert_gate,
    expert_up,
    expert_down,
    cotangent,
):
    tok_count = tokens.shape[0]
    here = expert_gate.shape[0]
    cube = lax.axis_size("dp") == 4 and lax.axis_size("expert") == 8 and here % 2 == 0
    plan = Cube(here) if cube else Plain(here)

    small = jnp.concatenate(
        [
            router_weight,
            first_gain[:, None],
            second_gain[:, None],
            jnp.zeros((router_weight.shape[0], 128 - EXPERTS - 2), BF16),
        ],
        axis=1,
    )
    grad_block = with_extra(cotangent, [routes.T.astype(F32)])
    grad_near = plan.spread(grad_block)
    dense_parts, lines = plan.gather_dense(
        jnp.concatenate([query_weight, key_weight, value_weight, output_weight, small], axis=1)
    )
    grad_across = plan.cross(grad_block)
    grad_far = plan.spread(tie(grad_across, dense_parts[-1][0]))
    shards = pack_weights(expert_gate, expert_up, expert_down)
    weights = [plan.weight(tie(shards, lines, grad_across), 0)]

    cosine, sine = layout_tables(lengths[0], tok_count)
    cosine, sine = jnp.concatenate([cosine, cosine], axis=1), jnp.concatenate([sine, sine], axis=1)
    kept = forward_call(lengths[0], tokens, dense_parts, cosine, sine)
    residual, normed_two, logits, dense = kept[6:]
    logits = logits[:, :EXPERTS]
    choose = (routes[:, :, None] == jnp.arange(EXPERTS, dtype=jnp.int32)[None, None, :]).astype(F32)
    chosen = jnp.sum(choose * logits[:, None, :], axis=-1)
    top_chosen = jnp.max(chosen, axis=-1, keepdims=True)
    raised_gates = jnp.exp(chosen - top_chosen)
    gates = raised_gates / jnp.sum(raised_gates, axis=-1, keepdims=True)

    gate_lines = gates.T
    gate_high = lax.optimization_barrier(gate_lines.astype(BF16))
    gate_low = gate_lines - gate_high.astype(F32)
    block, grad_near, grad_far, weights = lax.optimization_barrier(
        (with_extra(normed_two, [gate_high, gate_low]), grad_near, grad_far, weights)
    )
    rows_near, rows_across = lax.optimization_barrier((plan.spread(block), plan.cross(block)))
    rows = plan.both_cores(rows_near, plan.spread(rows_across))
    grad_rows = plan.both_cores(grad_near, grad_far)
    for e in range(1, plan.share):
        weights.append(plan.weight(tie(shards, rows_across, weights[-1]), e))

    done, weight_parts = None, []
    for e in range(plan.share):
        mixes, backs, weight_part = expert_call(
            plan.own_ids[e : e + 1].astype(jnp.int32),
            rows,
            grad_rows,
            weights[e],
            plan.shards,
            plan.turned,
            done,
        )
        done = (mixes, backs)
        if e < plan.share - 1:
            weight_parts.append([plan.weight_grad(weight_part, 0)])
        if e > 0:
            done, weight_parts[e - 1] = lax.optimization_barrier((done, weight_parts[e - 1]))
        if e < plan.share - 1:
            last = weight_part
    arrived = weight_parts
    if plan.share > 1:
        arrived[-1].append(plan.weight_grad(tie(last, arrived[-1]), 1))
    folded = plan.fold_once(plan.fold_cores(done[1]))
    mixes = plan.fold_cores(done[0])
    folded, mixes, arrived = lax.optimization_barrier((folded, mixes, arrived))
    folded = plan.fold_twice(folded)
    mixes = plan.fold_once(tie(mixes, folded))
    back_held = plan.fold_planes(folded)
    back_rows = back_held[:BLOCK]
    owners_back = back_held[BLOCK : BLOCK + EXTRA // 2] + back_held[BLOCK + EXTRA // 2 :]
    owners_back = owners_back.reshape(EXPERTS, BLOCK)
    arrived.append([plan.weight_grad(tie(weight_part, back_rows), 0)])

    gate_back = jnp.sum(choose * owners_back.T[:, None, :], axis=-1)
    chosen_back = gates * (gate_back - jnp.sum(gates * gate_back, axis=-1, keepdims=True))
    logit_back = jnp.sum(chosen_back[:, :, None] * choose, axis=1).astype(BF16)
    logit_back = jnp.pad(logit_back, ((0, 0), (0, 128 - EXPERTS)))
    input_grad, late, early = backward_call(
        lengths[0], tokens, cotangent, dense, cosine, sine, kept, logit_back, back_rows
    )
    late, early, mixes, arrived = lax.optimization_barrier((late, early, mixes, arrived))
    arrived[-1].append(plan.weight_grad(tie(weight_part, arrived[-1]), 1))
    sums, arrived = plan.fold_dense([late, early], arrived)
    mixture = plan.fold_planes(plan.fold_twice(tie(mixes, sums)))
    output = (residual + mixture[:BLOCK]).astype(BF16)
    dense_grad = plan.spread_dense(plan.sum_dense(sums))
    weight_grad = plan.weight_grads(arrived)
    return (
        output,
        input_grad,
        dense_grad[:, :HD],
        dense_grad[:, HD : HD + KVD],
        dense_grad[:, HD + KVD : QKV],
        dense_grad[:, QKV + 128 :],
        dense_grad[:, QKV : QKV + EXPERTS],
        dense_grad[:, QKV + EXPERTS],
        dense_grad[:, QKV + EXPERTS + 1],
        weight_grad[:, :, :FF],
        weight_grad[:, :, FF : 2 * FF],
        jnp.concatenate(
            jnp.split(weight_grad[:, :, 2 * FF :], FF // weight_grad.shape[1], axis=2), axis=1
        ),
    )


def solution(mesh):
    return jax.shard_map(
        on_device,
        mesh=mesh,
        in_specs=(
            P(("dp", "expert"), None),
            P(("dp", "expert"), None),
            P(("dp", "expert"), None),
            P("dp", None),
            P("dp", None),
            P("dp", None),
            P("dp", None),
            P("dp", None),
            P("dp"),
            P("dp"),
            P("expert", "dp", None),
            P("expert", "dp", None),
            P("expert", None, "dp"),
            P(("dp", "expert"), None),
        ),
        out_specs=(
            P(("dp", "expert"), None),
            P(("dp", "expert"), None),
            P("dp", None),
            P("dp", None),
            P("dp", None),
            P("dp", None),
            P("dp", None),
            P("dp"),
            P("dp"),
            P("expert", "dp", None),
            P("expert", "dp", None),
            P("expert", None, "dp"),
        ),
        check_vma=False,
    )
```
